32 devices in a mesh: group: 2 (over y), dp: 8 (over z, x), tensor: 2 (over core).
Axes of the slice: x: 2, y: 2, z: 4, core: 2. Of those that a mesh axis runs over, the one named last changes fastest.
Arguments:
- queries: bfloat16 [64, 32, 4096], P(('group', 'dp'), None, 'tensor'), parts along dimension 0, may hold values from -17 to 17
- response_cache: bfloat16 [64, 32, 2, 512], P(('group', 'dp'), None, None, 'tensor'), parts along dimension 0, may hold values from -6 to 6
- prefix_cache: bfloat16 [16, 224, 2, 512], P(('group', 'dp'), None, None, 'tensor'), parts along dimension 0, may hold values from -8 to 8
- upstream: bfloat16 [64, 32, 4096], P(('group', 'dp'), None, 'tensor'), parts along dimension 0, may hold values from -6 to 6
- reward_probe: float32 [4096], P('tensor'), may hold values from -1.5 to 1.5
- slot_offsets: int32 [16, 4], P(('group', 'dp')), parts along dimension 0, may hold values from -2 to 2, as said below
- partner: int32 [64], P('group'), parts along dimension 0, may hold values from 0 to 31, as said below
- labels: int32 [64], P('group'), parts along dimension 0, may hold values from 0 to 2
Outputs:
- rewards: float32 [64], P(('group', 'dp')), parts along dimension 0
- pair_loss: float32 [2], P('group'), parts along dimension 0
- grad_queries: bfloat16 [64, 32, 4096], P(('group', 'dp'), None, 'tensor'), parts along dimension 0
- grad_response: bfloat16 [64, 32, 2, 512], P(('group', 'dp'), None, None, 'tensor'), parts along dimension 0
- grad_prefix: bfloat16 [16, 224, 2, 512], P(('group', 'dp'), None, None, 'tensor'), parts along dimension 0
The draws below stay inside these ranges and needn't reach their ends.
There are 2 independent parts, one for each index of `group`. The reference program is written for one: setup_inputs(seed, part) draws one part's arguments, and reference() takes and returns one part's arrays. A program takes and returns all parts, laid end to end along the dimension named above; an argument that names none is the same for every part. Nothing has to cross between parts.
Inputs may be any that keep to these rules, and one draw needn't show every extreme that they name: `slot_offsets`: slots 0 and 1 of every device have offset 0. partner[i] differs from i and has the same prompt; the responses of one prompt name each other once around a cycle.
All inputs are finite; a program needn't handle non-finite values.
Results may differ from the reference program's by a relative error of at most 0.011.
Values may be sent and summed in bfloat16 or wider, within the bound.
A program may use at most 64 MiB of HBM per device.

```python
import math
import jax
import jax.numpy as jnp
from jax import lax

HQ = 32
KVH = 4
HD = 128
LP = 224
LR = 32
R_DEV = 4
SPAN = 2
PROMPTS = 8
RESP = 32
N_DP = 8


def slot_table(key):
    table_key = jax.random.fold_in(key, 202)
    raw = jax.random.randint(table_key, (PROMPTS, R_DEV), -SPAN, SPAN + 1, dtype=jnp.int32)
    row_ids = lax.broadcasted_iota(jnp.int32, (PROMPTS, R_DEV), 0)
    col_ids = lax.broadcasted_iota(jnp.int32, (PROMPTS, R_DEV), 1)
    raw = jnp.where(col_ids < 2, 0, raw)
    raw = jnp.where((row_ids == 0) & (col_ids == 2), -SPAN, raw)
    raw = jnp.where((row_ids == 0) & (col_ids == 3), SPAN, raw)
    return raw


def draw_queries(key, part):
    key = jax.random.fold_in(key, 3)
    base = jnp.clip(jax.random.normal(key, (RESP, LR, HQ * HD), jnp.float32) * 1.5, -9.0, 9.0)
    return base.astype(jnp.bfloat16)


def draw_prefix_cache(key, part):
    key = jax.random.fold_in(key, 4)
    base = jnp.clip(jax.random.normal(key, (PROMPTS, LP, 2, KVH * HD), jnp.float32), -6.0, 6.0)
    return base.astype(jnp.bfloat16)


def draw_slot_offsets(key, part):
    return slot_table(key)


def draw_partner(key, part):
    offsets = slot_table(key)
    key = jax.random.fold_in(key, 5)
    device_ids = jnp.arange(PROMPTS, dtype=jnp.int32)
    prompt_ids = ((device_ids[:, None] + offsets) % PROMPTS).reshape(-1)
    ranking = jax.random.permutation(key, RESP).astype(jnp.int32)
    order = jnp.argsort(prompt_ids * RESP + ranking).astype(jnp.int32)
    sorted_prompt = prompt_ids[order]
    positions = jnp.arange(RESP, dtype=jnp.int32)
    starts = (positions == 0) | (sorted_prompt != jnp.roll(sorted_prompt, 1))
    lasts = (positions == RESP - 1) | (sorted_prompt != jnp.roll(sorted_prompt, -1))
    group_start = lax.cummax(jnp.where(starts, positions, 0))
    following = jnp.where(lasts, group_start, positions + 1)
    partner_sorted = order[following]
    return jnp.zeros((RESP,), jnp.int32).at[order].set(partner_sorted)


def touch_ends(drawn, rng, least, high):
    dims = drawn.shape
    spot = [jax.random.randint(jax.random.fold_in(rng, axis), (), 0, dims[axis]) for axis in range(len(dims))]
    drawn = drawn.at[tuple(spot)].set(least)
    longest = dims.index(max(dims))
    spot[longest] = (spot[longest] + 1) % dims[longest]
    return drawn.at[tuple(spot)].set(high)


def block_levels(own_key, extent, cuts, low, high):
    gain = 1.0
    for dim, shards_of in cuts:
        heights = jax.random.uniform(jax.random.fold_in(jax.random.fold_in(own_key, 6), dim), (shards_of,), jnp.float32, low / len(cuts), high / len(cuts))
        gain = gain * jnp.repeat(jnp.exp(heights), extent[dim] // shards_of).reshape((-1,) + (1,) * (len(extent) - 1 - dim))
    return gain


def noise(key, dims, scale, reach, split=(), kind=jnp.bfloat16):
    drawn = scale * jax.random.normal(key, dims, jnp.float32)
    if split:
        drawn = drawn * block_levels(key, dims, split, -0.22, 0.18)
    return jnp.clip(drawn, -reach, reach).astype(kind)


def setup_inputs(seed: int = 0, part: int = 0) -> dict:
    key_list = jax.random.split(jax.random.key(seed), 9)
    own_keys = jax.random.split(jax.random.fold_in(key_list[8], part), 9)
    return {
        "queries": draw_queries(jax.random.fold_in(jax.random.fold_in(key_list[8], part), 71), part),
        "response_cache": noise(own_keys[1], (RESP, LR, 2, KVH * HD), 1.0, 6.0, ((0, 8), (3, 2))),
        "prefix_cache": draw_prefix_cache(jax.random.fold_in(jax.random.fold_in(key_list[8], part), 71), part),
        "upstream": noise(own_keys[3], (RESP, LR, HQ * HD), 1.0, 6.0, ((0, 8), (2, 2))),
        "reward_probe": noise(key_list[4], (HQ * HD,), 0.25, 1.5, ((0, 2),), jnp.float32),
        "slot_offsets": draw_slot_offsets(jax.random.fold_in(jax.random.fold_in(key_list[8], part), 71), part),
        "partner": draw_partner(jax.random.fold_in(jax.random.fold_in(key_list[8], part), 71), part),
        "labels": touch_ends(jax.random.randint(own_keys[7], (RESP,), 0, 3), jax.random.fold_in(own_keys[7], 1), 0, 2).astype(jnp.int32),
    }


highest = lax.Precision.HIGHEST

def davidson(reward_all, partner, labels):
    first_reward = reward_all
    second = reward_all[partner]
    middle = 0.5 * (first_reward + second)
    exp_first = jnp.exp(first_reward)
    exp_second = jnp.exp(second)
    exp_middle = jnp.exp(middle)
    totals = exp_first + exp_second + exp_middle
    chosen = jnp.where(labels == 0, first_reward, jnp.where(labels == 1, second, middle))
    loss_value = jnp.mean(jnp.log(totals) - chosen).reshape(1)
    tie_share = 0.5 * exp_middle / totals
    half_tie = jnp.where(labels == 2, 0.5, 0.0)
    grad_first = exp_first / totals + tie_share - jnp.where(labels == 0, 1.0, 0.0) - half_tie
    grad_second = exp_second / totals + tie_share - jnp.where(labels == 1, 1.0, 0.0) - half_tie
    indices = jnp.arange(first_reward.shape[0], dtype=jnp.int32)
    reward_grad = jnp.zeros_like(first_reward).at[indices].add(grad_first).at[partner].add(grad_second)
    return (loss_value, reward_grad)

def attend(queries_dev, response_dev, prefix_dev):
    group_size = HQ // KVH
    key_rows = jnp.concatenate([prefix_dev, response_dev], axis=1)
    total_keys = key_rows.shape[1]
    query_part = queries_dev.astype(jnp.float32).reshape(R_DEV, LR, KVH, group_size, HD)
    key_part = key_rows[:, :, 0].astype(jnp.float32).reshape(R_DEV, total_keys, KVH, HD)
    value_part = key_rows[:, :, 1].astype(jnp.float32).reshape(R_DEV, total_keys, KVH, HD)
    score_scale = 1.0 / math.sqrt(HD)
    scores = jnp.einsum('rtkgd,rnkd->rkgtn', query_part, key_part, precision=highest) * score_scale
    row_ids = lax.broadcasted_iota(jnp.int32, (LR, total_keys), 0)
    col_ids = lax.broadcasted_iota(jnp.int32, (LR, total_keys), 1)
    visible = (col_ids < LP) | (col_ids - LP <= row_ids)
    scores = jnp.where(visible, scores, -1e+30)
    row_top = lax.optimization_barrier(jnp.max(scores, axis=-1, keepdims=True))
    exp_scores = jnp.exp(scores - row_top)
    weights = exp_scores / lax.optimization_barrier(jnp.sum(exp_scores, axis=-1, keepdims=True))
    weights_low = lax.optimization_barrier(weights.astype(jnp.bfloat16))
    attended = jnp.einsum('rkgtn,rnkd->rtkgd', weights_low.astype(jnp.float32), value_part, precision=highest)
    return (query_part, key_part, value_part, weights, weights_low, attended)

def reference(queries, response_cache, prefix_cache, upstream, reward_probe, slot_offsets, partner, labels):
    query_width = HQ * HD
    kv_width = KVH * HD
    query_dev = queries.reshape(N_DP, R_DEV, LR, query_width)
    response_dev = response_cache.reshape(N_DP, R_DEV, LR, 2, kv_width)
    upstream_dev = upstream.reshape(N_DP, R_DEV, LR, query_width)
    device_ids = jnp.arange(N_DP, dtype=jnp.int32)
    prompt_ids = (device_ids[:, None] + slot_offsets) % N_DP

    def reward_of(inputs):
        queries_one, response_one, prompt_row = inputs
        attended = attend(queries_one, response_one, prefix_cache[prompt_row])[5]
        return lax.optimization_barrier(jnp.sum(attended.reshape(R_DEV, LR, query_width)[:, -1] * reward_probe, axis=-1))
    rewards = lax.map(reward_of, (query_dev, response_dev, prompt_ids)).reshape(-1)
    loss_value, reward_grad = davidson(rewards, partner, labels)
    grad_dev = reward_grad.reshape(N_DP, R_DEV)
    reach_count = 2 * SPAN + 1

    def backward_step(total, inputs):
        queries_one, response_one, upstream_one, prompt_row, grad_row, device_id, offset_row = inputs
        query_part, key_part, value_part, weights, weights_low, attended = attend(queries_one, response_one, prefix_cache[prompt_row])
        group_size = HQ // KVH
        d_attended = upstream_one.astype(jnp.float32).at[:, -1].add(grad_row[:, None] * reward_probe)
        d_attended = lax.optimization_barrier(d_attended.astype(jnp.bfloat16))
        d_part = d_attended.astype(jnp.float32).reshape(R_DEV, LR, KVH, group_size, HD)
        d_weights = jnp.einsum('rtkgd,rnkd->rkgtn', d_part, value_part, precision=highest)
        row_delta = jnp.transpose(lax.optimization_barrier(jnp.sum(d_part * attended, axis=-1)), (0, 2, 3, 1))[..., None]
        score_scale = 1.0 / math.sqrt(HD)
        d_scores = lax.optimization_barrier((weights * (d_weights - row_delta) * score_scale).astype(jnp.bfloat16))
        d_scores = d_scores.astype(jnp.float32)
        d_query = jnp.einsum('rkgtn,rnkd->rtkgd', d_scores, key_part, precision=highest)
        d_query = d_query.reshape(R_DEV, LR, query_width).astype(jnp.bfloat16)
        d_key = jnp.einsum('rkgtn,rtkgd->rnkd', d_scores, query_part, precision=highest)
        d_value = jnp.einsum('rkgtn,rtkgd->rnkd', weights_low.astype(jnp.float32), d_part, precision=highest)
        total_keys = d_key.shape[1]
        d_rows = jnp.stack([d_key.reshape(R_DEV, total_keys, kv_width), d_value.reshape(R_DEV, total_keys, kv_width)], axis=2)
        d_resp = d_rows[:, LP:].astype(jnp.bfloat16)
        selector = (offset_row[:, None] + SPAN == jnp.arange(reach_count, dtype=jnp.int32)[None, :]).astype(jnp.float32)
        by_reach = jnp.einsum('rm,rlck->mlck', selector, d_rows[:, :LP], precision=highest).astype(jnp.bfloat16)
        targets = (device_id + jnp.arange(-SPAN, SPAN + 1, dtype=jnp.int32)) % N_DP
        total = total.at[targets].add(by_reach.astype(jnp.float32))
        return (total, (d_query, d_resp))
    initial = jnp.zeros((N_DP, LP, 2, kv_width), jnp.float32)
    total, (grad_q, grad_r) = lax.scan(backward_step, initial, (query_dev, response_dev, upstream_dev, prompt_ids, grad_dev, device_ids, slot_offsets))
    grad_queries = grad_q.reshape(RESP, LR, query_width)
    grad_response = grad_r.reshape(RESP, LR, 2, kv_width)
    return (rewards, loss_value, grad_queries, grad_response, total.astype(jnp.bfloat16))
```

```python
import functools
import math

import jax
import jax.numpy as jnp
from jax import lax
from jax.experimental import pallas as pl
from jax.experimental.pallas import tpu as pltpu
from jax.sharding import PartitionSpec as P

HD = 128
SPAN = 2
LAST_ROWS = 16
MESH = pl.DeviceIdType.MESH


def dot(a, b, contract_a, contract_b):
    return lax.dot_general(
        a, b, (((contract_a,), (contract_b,)), ((), ())), preferred_element_type=jnp.float32
    )


def kernel(
    n_dp,
    n_tensor,
    offsets,
    queries_hbm,
    upstream_hbm,
    prefix,
    response,
    probe,
    partner,
    labels,
    rewards_out,
    loss_out,
    grad_q_hbm,
    grad_r_out,
    grad_p_out,
    q_buf,
    up_buf,
    gq_buf,
    near0,
    near1,
    near2,
    near3,
    d_rows,
    w_last,
    p_last,
    o_last,
    q_last,
    message,
    table,
    reward_sum,
    out_a,
    out_b,
    out_c,
    out_d,
    in_a,
    in_b,
    in_c,
    in_d,
    local_sem,
    fwd_send,
    fwd_recv,
    bwd_send,
    bwd_recv,
    rew_send,
    rew_recv,
):
    slots, rows, width = q_buf.shape
    chunks, prefix_len, _ = prefix.shape
    heads_kv = chunks // 2
    group = width // HD // heads_kv
    keys = prefix_len + rows
    m_len = group * rows
    near = (near0, near1, near2, near3)
    scale = 1.0 / math.sqrt(HD)

    me = lax.axis_index("dp")
    my_t = lax.axis_index("tensor")
    odd = lax.rem(me, 2)
    mate = me + 1 - 2 * odd
    ahead = lax.rem(me + 2, n_dp)
    behind = lax.rem(me + n_dp - 2, n_dp)
    n_all = n_dp * n_tensor
    my_all = me * n_tensor + my_t

    def place(step):
        other = lax.rem(my_all + step, n_all)
        return {"dp": lax.div(other, n_tensor), "tensor": lax.rem(other, n_tensor)}

    load_q = pltpu.make_async_copy(queries_hbm, q_buf, local_sem.at[0])
    load_up = pltpu.make_async_copy(upstream_hbm, up_buf, local_sem.at[1])
    load_q.start()
    load_up.start()

    barrier = pltpu.get_barrier_semaphore()

    def greet(step, carry):
        pl.semaphore_signal(barrier, inc=1, device_id=place(step), device_id_type=MESH)
        return carry

    lax.fori_loop(1, n_all, greet, 0)
    pl.semaphore_wait(barrier, n_all - 1)

    def forward_copy(chunk, kind):
        if kind == 0:
            src, dst, to = prefix.at[chunk], near[chunk].at[1 + 2 * odd], mate
        elif kind == 1:
            src, dst, to = prefix.at[chunk], near[chunk].at[0], ahead
        elif kind == 2:
            src, dst, to = prefix.at[chunk], near[chunk].at[4], behind
        else:
            src, dst, to = near[chunk].at[4 - 4 * odd], near[chunk].at[3 - 2 * odd], mate
        return pltpu.make_async_remote_copy(
            src_ref=src,
            dst_ref=dst,
            send_sem=fwd_send.at[chunk, kind],
            recv_sem=fwd_recv.at[chunk, kind],
            device_id={"dp": to},
            device_id_type=MESH,
        )

    fwd = [[forward_copy(c, k) for k in range(4)] for c in range(chunks)]
    for c in range(chunks):
        for k in (1, 2, 0):
            fwd[c][k].start()

    lane = lax.broadcasted_iota(jnp.int32, (1, m_len), 1)
    token = lax.rem(lane, rows)
    not_last = jnp.where(token == rows - 1, 0.0, 1.0)
    causal = lax.broadcasted_iota(jnp.int32, (rows, m_len), 0) <= lax.rem(
        lax.broadcasted_iota(jnp.int32, (rows, m_len), 1), rows
    )
    pick = jnp.where(
        lax.broadcasted_iota(jnp.int32, (LAST_ROWS, m_len), 0) * rows + (rows - 1)
        == lax.broadcasted_iota(jnp.int32, (LAST_ROWS, m_len), 1),
        1.0,
        0.0,
    ).astype(jnp.bfloat16)

    def stacked(buf, r, g):
        return jnp.concatenate(
            [buf[r, :, (g * group + h) * HD : (g * group + h + 1) * HD] for h in range(group)],
            axis=0,
        )

    def key_value(r, g, prefix_k, prefix_v):
        mine = pl.ds(pl.multiple_of(r * rows, rows), rows)
        return (
            jnp.concatenate([prefix_k, response[2 * g, mine]], axis=0),
            jnp.concatenate([prefix_v, response[2 * g + 1, mine]], axis=0),
        )

    def probe_of(g):
        return jnp.concatenate(
            [probe[g * group : (g + 1) * group], jnp.zeros((LAST_ROWS - group, HD), jnp.float32)],
            axis=0,
        )

    def last_token(r, g, k, v):
        q31 = dot(pick, stacked(q_buf, r, g), 1, 0).astype(jnp.bfloat16)
        s = dot(q31, k, 1, 1)
        e = jnp.exp((s - jnp.max(s, axis=1, keepdims=True)) * scale)
        w = e / jnp.sum(e, axis=1, keepdims=True)
        w_low = w.astype(jnp.bfloat16)
        o = dot(w_low, v, 1, 0)
        q_last[r, g] = q31
        w_last[r, g] = w_low
        p_last[r, g] = w
        o_last[r, g] = o
        return jnp.sum(
            jnp.sum(o * probe_of(g), axis=0, keepdims=True), axis=1, keepdims=True
        )

    def main(r, g, k, v):
        q = stacked(q_buf, r, g)
        d_out = stacked(up_buf, r, g)
        s = dot(k, q, 1, 1)
        s = jnp.concatenate(
            [s[:prefix_len], jnp.where(causal, s[prefix_len:], -1e30)], axis=0
        )
        e = jnp.exp((s - jnp.max(s, axis=0, keepdims=True)) * scale)
        w = e * (not_last / jnp.sum(e, axis=0, keepdims=True))
        w_low = w.astype(jnp.bfloat16)
        dw = dot(v, d_out, 1, 1)
        delta = jnp.sum(w_low.astype(jnp.float32) * dw, axis=0, keepdims=True)
        ds = (w * (dw - delta) * scale).astype(jnp.bfloat16)
        d_rows[r, 2 * g] = dot(ds, q, 1, 0)
        d_rows[r, 2 * g + 1] = dot(w_low, d_out, 1, 0)
        dq = dot(ds, k, 0, 0).astype(jnp.bfloat16)
        for h in range(group):
            gq_buf[r, :, (g * group + h) * HD : (g * group + h + 1) * HD] = dq[
                h * rows : (h + 1) * rows
            ]

    slot_row = lax.broadcasted_iota(jnp.int32, (8, HD), 0)

    load_q.wait()
    load_up.wait()

    def near_slot(r, note):
        for g in range(heads_kv):
            k, v = key_value(r, g, prefix[2 * g], prefix[2 * g + 1])
            note = note + jnp.where(slot_row == r, last_token(r, g, k, v), 0.0)
            main(r, g, k, v)
        return note

    note = lax.fori_loop(0, 2, near_slot, jnp.zeros((8, HD), jnp.float32))
    for c in range(chunks):
        near[c][2] = prefix[c]

    for c in range(chunks):
        kind = 2 - odd
        pltpu.make_async_remote_copy(
            src_ref=prefix.at[c],
            dst_ref=near[c].at[4 - 4 * odd],
            send_sem=fwd_send.at[c, kind],
            recv_sem=fwd_recv.at[c, kind],
            device_id={"dp": mate},
            device_id_type=MESH,
        ).wait_recv()
        fwd[c][3].start()
    for c in range(chunks):
        kind = 1 + odd
        pltpu.make_async_remote_copy(
            src_ref=prefix.at[c],
            dst_ref=near[c].at[4 * odd],
            send_sem=fwd_send.at[c, kind],
            recv_sem=fwd_recv.at[c, kind],
            device_id={"dp": mate},
            device_id_type=MESH,
        ).wait_recv()
        fwd[c][0].wait_recv()
        fwd[c][3].wait_recv()

    def far_keys(r, g):
        reach = offsets[0, r] + SPAN
        return key_value(r, g, near[2 * g][reach], near[2 * g + 1][reach])

    def far_reward(r, note):
        for g in range(heads_kv):
            k, v = far_keys(r, g)
            note = note + jnp.where(slot_row == r, last_token(r, g, k, v), 0.0)
        return note

    note = lax.fori_loop(2, slots, far_reward, note)
    message[...] = note
    table[my_all] = note

    def reward_copy(step):
        return pltpu.make_async_remote_copy(
            src_ref=message,
            dst_ref=table.at[my_all],
            send_sem=rew_send.at[step],
            recv_sem=rew_recv.at[step],
            device_id=place(step),
            device_id_type=MESH,
        )

    def tell(step, carry):
        reward_copy(step).start()
        return carry

    lax.fori_loop(1, n_all, tell, 0)

    def far_slot(r, carry):
        for g in range(heads_kv):
            k, v = far_keys(r, g)
            main(r, g, k, v)
        return carry

    lax.fori_loop(2, slots, far_slot, 0)

    def hear(step, carry):
        reward_copy(step).wait()
        return carry

    lax.fori_loop(1, n_all, hear, 0)

    summed = jnp.sum(table[...].reshape(n_dp, n_tensor, 8, HD), axis=1).reshape(n_dp * 8, HD)
    reward_sum[...] = summed
    resp = partner.shape[1]
    other = partner[...]
    label = labels[...]
    all_rows = lax.broadcasted_iota(jnp.int32, (n_dp * 8, resp), 0)
    all_ids = lax.rem(all_rows, 8) + lax.div(all_rows, 8) * slots
    all_ids = jnp.where(lax.rem(all_rows, 8) < slots, all_ids, -1)
    pair = lax.broadcasted_iota(jnp.int32, (n_dp * 8, resp), 1)
    column = summed[:, :1]
    first = jnp.sum(jnp.where(all_ids == pair, column, 0.0), axis=0, keepdims=True)
    second = jnp.sum(jnp.where(all_ids == other, column, 0.0), axis=0, keepdims=True)
    middle = 0.5 * (first + second)
    exp_first = jnp.exp(first)
    exp_second = jnp.exp(second)
    exp_middle = jnp.exp(middle)
    totals = exp_first + exp_second + exp_middle
    chosen = jnp.where(label == 0, first, jnp.where(label == 1, second, middle))
    loss = jnp.sum(jnp.log(totals) - chosen, axis=1, keepdims=True) * (1.0 / resp)
    loss_out[0] = loss[0, 0]
    tie_share = 0.5 * exp_middle / totals
    half_tie = jnp.where(label == 2, 0.5, 0.0)
    grad_first = exp_first / totals + tie_share - jnp.where(label == 0, 1.0, 0.0) - half_tie
    grad_second = exp_second / totals + tie_share - jnp.where(label == 1, 1.0, 0.0) - half_tie
    my_rows = lax.broadcasted_iota(jnp.int32, (8, resp), 0)
    my_ids = jnp.where(my_rows < slots, my_rows + me * slots, -1)
    my_pair = lax.broadcasted_iota(jnp.int32, (8, resp), 1)
    grads = jnp.sum(
        jnp.where(my_ids == my_pair, grad_first, 0.0) + jnp.where(my_ids == other, grad_second, 0.0),
        axis=1,
        keepdims=True,
    )
    own = reward_sum[pl.ds(pl.multiple_of(me * 8, 8), 8)]
    for j in range(slots):
        rewards_out[j] = own[j, 0]

    def finish(r, g, k, v):
        mine = jnp.sum(
            jnp.where(slot_row[:, :1] == r, grads, 0.0), axis=0, keepdims=True
        )
        up31 = dot(pick, stacked(up_buf, r, g), 1, 0)
        d31 = (up31 + mine * probe_of(g)).astype(jnp.bfloat16)
        dw = dot(d31, v, 1, 1)
        delta = jnp.sum(d31.astype(jnp.float32) * o_last[r, g], axis=1, keepdims=True)
        ds = (p_last[r, g] * (dw - delta) * scale).astype(jnp.bfloat16)
        dk = d_rows[r, 2 * g] + dot(ds, q_last[r, g], 0, 0)
        dv = d_rows[r, 2 * g + 1] + dot(w_last[r, g], d31, 0, 0)
        dq = dot(pick, dot(ds, k, 1, 0).astype(jnp.bfloat16), 0, 0).astype(jnp.bfloat16)
        for h in range(group):
            cols = slice((g * group + h) * HD, (g * group + h + 1) * HD)
            gq_buf[r, :, cols] = gq_buf[r, :, cols] + dq[h * rows : (h + 1) * rows]
        mine_rows = pl.ds(pl.multiple_of(r * rows, rows), rows)
        grad_r_out[2 * g, mine_rows] = dk[prefix_len:].astype(jnp.bfloat16)
        grad_r_out[2 * g + 1, mine_rows] = dv[prefix_len:].astype(jnp.bfloat16)
        return dk[:prefix_len], dv[:prefix_len]

    def backward_copy(chunk, kind):
        src = (out_a, out_b, out_c, out_d)[kind].at[chunk]
        dst = (in_a, in_b, in_c, in_d)[kind].at[chunk]
        if kind < 2:
            to = mate
        elif kind == 2:
            to = lax.rem(me + n_dp + 4 * odd - 2, n_dp)
        else:
            to = lax.rem(me + n_dp + 2 - 4 * odd, n_dp)
        return pltpu.make_async_remote_copy(
            src_ref=src,
            dst_ref=dst,
            send_sem=bwd_send.at[chunk, kind],
            recv_sem=bwd_recv.at[chunk, kind],
            device_id={"dp": to},
            device_id_type=MESH,
        )

    bwd = [[backward_copy(c, k) for k in range(4)] for c in range(chunks)]
    reach2 = offsets[0, 2]
    reach3 = offsets[0, 3]

    def part(d2, d3, reach):
        return jnp.where(reach2 == reach, d2, 0.0) + jnp.where(reach3 == reach, d3, 0.0)

    for g in range(heads_kv):
        pairs = [finish(r, g, *far_keys(r, g)) for r in (2, 3)]
        for c in range(2):
            chunk = 2 * g + c
            d2, d3 = pairs[0][c], pairs[1][c]
            out_a[chunk] = part(d2, d3, 2 * odd - 1).astype(jnp.bfloat16)
            bwd[chunk][0].start()
            out_c[chunk] = part(d2, d3, 4 * odd - 2).astype(jnp.bfloat16)
            bwd[chunk][2].start()
            out_b[chunk] = part(d2, d3, 1 - 2 * odd).astype(jnp.bfloat16)
            bwd[chunk][1].start()
            d_rows[2, chunk, :prefix_len] = part(d2, d3, 0)
            d_rows[3, chunk, :prefix_len] = part(d2, d3, 2 - 4 * odd)

    for c in range(chunks):
        bwd[c][0].wait_recv()
        out_d[c] = (
            d_rows[3, c, :prefix_len] + in_a[c].astype(jnp.float32)
        ).astype(jnp.bfloat16)
        bwd[c][3].start()

    for g in range(heads_kv):
        for r in (0, 1):
            k, v = key_value(r, g, prefix[2 * g], prefix[2 * g + 1])
            dk, dv = finish(r, g, k, v)
            d_rows[2, 2 * g, :prefix_len] += dk
            d_rows[2, 2 * g + 1, :prefix_len] += dv
    store_q = pltpu.make_async_copy(gq_buf, grad_q_hbm, local_sem.at[2])
    store_q.start()

    for c in range(chunks):
        bwd[c][1].wait_recv()
        bwd[c][2].wait_recv()
        bwd[c][3].wait_recv()
        grad_p_out[c] = (
            d_rows[2, c, :prefix_len]
            + in_b[c].astype(jnp.float32)
            + in_c[c].astype(jnp.float32)
            + in_d[c].astype(jnp.float32)
        ).astype(jnp.bfloat16)

    for c in range(chunks):
        for k in range(4):
            fwd[c][k].wait_send()
            bwd[c][k].wait_send()
    store_q.wait()


def per_device(
    n_dp,
    n_tensor,
    queries,
    response_cache,
    prefix_cache,
    upstream,
    reward_probe,
    slot_offsets,
    partner,
    labels,
):
    slots, rows, width = queries.shape
    prefix_len = prefix_cache.shape[1]
    kv_heads = response_cache.shape[3] // HD
    chunks = 2 * kv_heads
    keys = prefix_len + rows
    resp = partner.shape[0]
    n_all = n_dp * n_tensor
    prefix = prefix_cache.reshape(prefix_len, 2, kv_heads, HD).transpose(2, 1, 0, 3)
    prefix = prefix.reshape(chunks, prefix_len, HD)
    response = response_cache.reshape(slots * rows, 2, kv_heads, HD).transpose(2, 1, 0, 3)
    response = response.reshape(chunks, slots * rows, HD)
    vmem = pl.BlockSpec(memory_space=pltpu.VMEM)
    smem = pl.BlockSpec(memory_space=pltpu.SMEM)
    hbm = pl.BlockSpec(memory_space=pl.ANY)
    near = pltpu.VMEM((2 * SPAN + 1, prefix_len, HD), jnp.bfloat16)
    block = pltpu.VMEM((chunks, prefix_len, HD), jnp.bfloat16)
    rewards, loss, grad_q, grad_r, grad_p = pl.pallas_call(
        functools.partial(kernel, n_dp, n_tensor),
        out_shape=(
            jax.ShapeDtypeStruct((slots,), jnp.float32),
            jax.ShapeDtypeStruct((1,), jnp.float32),
            jax.ShapeDtypeStruct(queries.shape, jnp.bfloat16),
            jax.ShapeDtypeStruct((chunks, slots * rows, HD), jnp.bfloat16),
            jax.ShapeDtypeStruct((chunks, prefix_len, HD), jnp.bfloat16),
        ),
        in_specs=[smem, hbm, hbm, vmem, vmem, vmem, vmem, vmem],
        out_specs=(smem, smem, hbm, vmem, vmem),
        scratch_shapes=[
            pltpu.VMEM(queries.shape, jnp.bfloat16),
            pltpu.VMEM(queries.shape, jnp.bfloat16),
            pltpu.VMEM(queries.shape, jnp.bfloat16),
            near,
            near,
            near,
            near,
            pltpu.VMEM((slots, chunks, keys, HD), jnp.float32),
            pltpu.VMEM((slots, kv_heads, LAST_ROWS, keys), jnp.bfloat16),
            pltpu.VMEM((slots, kv_heads, LAST_ROWS, keys), jnp.float32),
            pltpu.VMEM((slots, kv_heads, LAST_ROWS, HD), jnp.float32),
            pltpu.VMEM((slots, kv_heads, LAST_ROWS, HD), jnp.bfloat16),
            pltpu.VMEM((8, HD), jnp.float32),
            pltpu.VMEM((n_all, 8, HD), jnp.float32),
            pltpu.VMEM((n_dp * 8, HD), jnp.float32),
            block,
            block,
            block,
            block,
            block,
            block,
            block,
            block,
            pltpu.SemaphoreType.DMA((3,)),
            pltpu.SemaphoreType.DMA((chunks, 4)),
            pltpu.SemaphoreType.DMA((chunks, 4)),
            pltpu.SemaphoreType.DMA((chunks, 4)),
            pltpu.SemaphoreType.DMA((chunks, 4)),
            pltpu.SemaphoreType.DMA((n_all,)),
            pltpu.SemaphoreType.DMA((n_all,)),
        ],
        compiler_params=pltpu.CompilerParams(
            collective_id=0, has_side_effects=True, vmem_limit_bytes=40 * 1024 * 1024
        ),
    )(
        slot_offsets,
        queries,
        upstream,
        prefix,
        response,
        reward_probe.reshape(width // HD, HD),
        partner.reshape(1, resp),
        labels.reshape(1, resp),
    )
    grad_response = grad_r.reshape(kv_heads, 2, slots, rows, HD).transpose(2, 3, 1, 0, 4)
    grad_prefix = grad_p.reshape(kv_heads, 2, 1, prefix_len, HD).transpose(2, 3, 1, 0, 4)
    return (
        rewards,
        loss,
        grad_q,
        grad_response.reshape(response_cache.shape),
        grad_prefix.reshape(prefix_cache.shape),
    )


def solution(mesh):
    in_specs = (
        P(("group", "dp"), None, "tensor"),
        P(("group", "dp"), None, None, "tensor"),
        P(("group", "dp"), None, None, "tensor"),
        P(("group", "dp"), None, "tensor"),
        P("tensor"),
        P(("group", "dp"), None),
        P("group"),
        P("group"),
    )
    out_specs = (
        P(("group", "dp")),
        P("group"),
        P(("group", "dp"), None, "tensor"),
        P(("group", "dp"), None, None, "tensor"),
        P(("group", "dp"), None, None, "tensor"),
    )
    return jax.shard_map(
        functools.partial(per_device, mesh.shape["dp"], mesh.shape["tensor"]),
        mesh=mesh,
        in_specs=in_specs,
        out_specs=out_specs,
        check_vma=False,
    )
```

```python
import functools
import math

import jax
import jax.numpy as jnp
from jax import lax
from jax.experimental import pallas as pl
from jax.experimental.pallas import tpu as pltpu
from jax.sharding import PartitionSpec as P

HD = 128
SPAN = 2
LAST_ROWS = 16
MESH = pl.DeviceIdType.MESH


def dot(a, b, contract_a, contract_b):
    return lax.dot_general(
        a, b, (((contract_a,), (contract_b,)), ((), ())), preferred_element_type=jnp.float32
    )


def kernel(
    n_dp,
    n_tensor,
    offsets,
    queries_hbm,
    upstream_hbm,
    prefix,
    response,
    probe,
    partner,
    labels,
    rewards_out,
    loss_out,
    grad_q_hbm,
    grad_r_out,
    grad_p_out,
    q_buf,
    up_buf,
    gq_buf,
    near0,
    near1,
    near2,
    near3,
    d_rows,
    w_last,
    p_last,
    o_last,
    q_last,
    message,
    table,
    reward_sum,
    sent_rows,
    got_rows,
    sent_stats,
    got_stats,
    stats_near,
    out_a,
    out_b,
    out_c,
    out_d,
    in_a,
    in_b,
    in_c,
    in_d,
    local_sem,
    fwd_send,
    fwd_recv,
    bwd_send,
    bwd_recv,
    rew_send,
    rew_recv,
    note_send,
    note_recv,
):
    slots, rows, width = q_buf.shape
    _, prefix_len, kv_width = prefix.shape
    heads_kv = kv_width // HD
    chunks = 2 * heads_kv
    group = width // HD // heads_kv
    keys = prefix_len + rows
    m_len = group * rows
    near = (near0, near1, near2, near3)
    scale = 1.0 / math.sqrt(HD)

    me = lax.axis_index("dp")
    my_t = lax.axis_index("tensor")
    odd = lax.rem(me, 2)
    mate = me + 1 - 2 * odd
    ahead = lax.rem(me + 2, n_dp)
    behind = lax.rem(me + n_dp - 2, n_dp)
    n_all = n_dp * n_tensor
    my_all = me * n_tensor + my_t

    def place(step):
        other = lax.rem(my_all + step, n_all)
        return {"dp": lax.div(other, n_tensor), "tensor": lax.rem(other, n_tensor)}

    load_q = pltpu.make_async_copy(queries_hbm, q_buf, local_sem.at[0])
    load_up = pltpu.make_async_copy(upstream_hbm, up_buf, local_sem.at[1])
    load_q.start()
    load_up.start()

    barrier = pltpu.get_barrier_semaphore()

    def greet(step, carry):
        pl.semaphore_signal(barrier, inc=1, device_id=place(step), device_id_type=MESH)
        return carry

    lax.fori_loop(1, n_all, greet, 0)
    pl.semaphore_wait(barrier, n_all - 1)

    def head(g):
        return slice(g * HD, (g + 1) * HD)

    def prefix_at(chunk):
        return prefix.at[chunk % 2, :, head(chunk // 2)]

    def forward_copy(chunk, kind):
        if kind == 0:
            src, dst, to = prefix_at(chunk), near[chunk].at[1 + 2 * odd], mate
        elif kind == 1:
            src, dst, to = prefix_at(chunk), near[chunk].at[0], ahead
        elif kind == 2:
            src, dst, to = prefix_at(chunk), near[chunk].at[4], behind
        else:
            src, dst, to = near[chunk].at[4 - 4 * odd], near[chunk].at[3 - 2 * odd], mate
        return pltpu.make_async_remote_copy(
            src_ref=src,
            dst_ref=dst,
            send_sem=fwd_send.at[chunk, kind],
            recv_sem=fwd_recv.at[chunk, kind],
            device_id={"dp": to},
            device_id_type=MESH,
        )

    fwd = [[forward_copy(c, k) for k in range(4)] for c in range(chunks)]
    for c in range(chunks):
        for k in (1, 2, 0):
            fwd[c][k].start()

    lane = lax.broadcasted_iota(jnp.int32, (1, m_len), 1)
    token = lax.rem(lane, rows)
    not_last = jnp.where(token == rows - 1, 0.0, 1.0)
    causal = lax.broadcasted_iota(jnp.int32, (rows, m_len), 0) <= lax.rem(
        lax.broadcasted_iota(jnp.int32, (rows, m_len), 1), rows
    )
    pick = jnp.where(
        lax.broadcasted_iota(jnp.int32, (LAST_ROWS, m_len), 0) * rows + (rows - 1)
        == lax.broadcasted_iota(jnp.int32, (LAST_ROWS, m_len), 1),
        1.0,
        0.0,
    ).astype(jnp.bfloat16)

    def stacked(buf, r, g):
        return jnp.concatenate(
            [buf[r, :, (g * group + h) * HD : (g * group + h + 1) * HD] for h in range(group)],
            axis=0,
        )

    def key_value(r, g, prefix_k, prefix_v):
        mine = pl.ds(pl.multiple_of(r * rows, rows), rows)
        return (
            jnp.concatenate([prefix_k, response[0, mine, head(g)]], axis=0),
            jnp.concatenate([prefix_v, response[1, mine, head(g)]], axis=0),
        )

    def probe_of(g):
        return jnp.concatenate(
            [probe[g * group : (g + 1) * group], jnp.zeros((LAST_ROWS - group, HD), jnp.float32)],
            axis=0,
        )

    def last_token(r, g, k, v):
        q31 = dot(pick, stacked(q_buf, r, g), 1, 0).astype(jnp.bfloat16)
        s = dot(q31, k, 1, 1)
        e = jnp.exp((s - jnp.max(s, axis=1, keepdims=True)) * scale)
        w = e / jnp.sum(e, axis=1, keepdims=True)
        w_low = w.astype(jnp.bfloat16)
        o = dot(w_low, v, 1, 0)
        q_last[r, g] = q31
        w_last[r, g] = w_low
        p_last[r, g] = w
        o_last[r, g] = o
        by_head = jnp.sum(o * probe_of(g), axis=1, keepdims=True)
        stats = [
            jnp.max(s, axis=1, keepdims=True),
            1.0 / jnp.sum(e, axis=1, keepdims=True),
            jnp.sum(o * dot(pick, stacked(up_buf, r, g), 1, 0), axis=1, keepdims=True),
            by_head,
        ]
        packed = jnp.zeros((LAST_ROWS, HD), jnp.float32)
        for i, stat in enumerate(stats):
            packed = packed + jnp.where(lane_of == g * len(stats) + i, stat, 0.0)
        return jnp.sum(by_head, axis=0, keepdims=True), packed

    def main(r, g, k, v):
        q = stacked(q_buf, r, g)
        d_out = stacked(up_buf, r, g)
        s = dot(k, q, 1, 1)
        s = jnp.concatenate(
            [s[:prefix_len], jnp.where(causal, s[prefix_len:], -1e30)], axis=0
        )
        e = jnp.exp((s - jnp.max(s, axis=0, keepdims=True)) * scale)
        w = e * (not_last / jnp.sum(e, axis=0, keepdims=True))
        w_low = w.astype(jnp.bfloat16)
        dw = dot(v, d_out, 1, 1)
        delta = jnp.sum(w_low.astype(jnp.float32) * dw, axis=0, keepdims=True)
        ds = (w * (dw - delta) * scale).astype(jnp.bfloat16)
        d_rows[r, 2 * g] = dot(ds, q, 1, 0)
        d_rows[r, 2 * g + 1] = dot(w_low, d_out, 1, 0)
        dq = dot(ds, k, 0, 0).astype(jnp.bfloat16)
        for h in range(group):
            gq_buf[r, :, (g * group + h) * HD : (g * group + h + 1) * HD] = dq[
                h * rows : (h + 1) * rows
            ]

    slot_row = lax.broadcasted_iota(jnp.int32, (8, HD), 0)
    lane_of = lax.broadcasted_iota(jnp.int32, (LAST_ROWS, HD), 1)

    load_q.wait()
    load_up.wait()

    for g in range(heads_kv):
        for i, buf in enumerate((q_buf, up_buf)):
            both = [dot(pick, stacked(buf, r, g), 1, 0)[:group] for r in (2, 3)]
            sent_rows[i, g] = jnp.concatenate(both, axis=0).astype(jnp.bfloat16)

    def note_copy(which, to):
        src = (sent_rows, sent_stats)[which]
        dst = (got_rows, got_stats)[which].at[to]
        near_by = (1, n_dp - 1, 2, n_dp - 2)[to]
        return pltpu.make_async_remote_copy(
            src_ref=src,
            dst_ref=dst,
            send_sem=note_send.at[which, to],
            recv_sem=note_recv.at[which, to],
            device_id={"dp": lax.rem(me + near_by, n_dp)},
            device_id_type=MESH,
        )

    notes = [[note_copy(which, to) for to in range(4)] for which in range(2)]

    note = jnp.zeros((8, HD), jnp.float32)
    own_stats = []
    for r in (0, 1):
        mine = jnp.zeros((LAST_ROWS, HD), jnp.float32)
        for g in range(heads_kv):
            k, v = key_value(r, g, prefix[0, :, head(g)], prefix[1, :, head(g)])
            reward, packed = last_token(r, g, k, v)
            note = note + jnp.where(slot_row == r, reward, 0.0)
            mine = mine + packed
            main(r, g, k, v)
        own_stats.append(mine[:group])
        if r == 0:
            for c in range(chunks):
                near[c][2] = prefix[c % 2, :, head(c // 2)]
    stats_near[...] = jnp.concatenate(own_stats, axis=0)

    def wait_arrival(c, kind, index):
        pltpu.make_async_remote_copy(
            src_ref=prefix_at(c),
            dst_ref=near[c].at[index],
            send_sem=fwd_send.at[c, kind],
            recv_sem=fwd_recv.at[c, kind],
            device_id={"dp": mate},
            device_id_type=MESH,
        ).wait_recv()

    for c in range(chunks):
        wait_arrival(c, 2 - odd, 4 - 4 * odd)
        fwd[c][3].start()
    for to in range(4):
        notes[0][to].start()

    def backward_copy(chunk, kind):
        src = (out_a, out_b, out_c, out_d)[kind].at[chunk]
        dst = (in_a, in_b, in_c, in_d)[kind].at[chunk]
        if kind < 2:
            to = mate
        elif kind == 2:
            to = lax.rem(me + n_dp + 4 * odd - 2, n_dp)
        else:
            to = lax.rem(me + n_dp + 2 - 4 * odd, n_dp)
        return pltpu.make_async_remote_copy(
            src_ref=src,
            dst_ref=dst,
            send_sem=bwd_send.at[chunk, kind],
            recv_sem=bwd_recv.at[chunk, kind],
            device_id={"dp": to},
            device_id_type=MESH,
        )

    bwd = [[backward_copy(c, k) for k in range(4)] for c in range(chunks)]
    reach2 = offsets[0, 2]
    reach3 = offsets[0, 3]

    def far_keys(r, g):
        reach = offsets[0, r] + SPAN
        return key_value(r, g, near[2 * g][reach], near[2 * g + 1][reach])

    def part(d2, d3, reach):
        return jnp.where(reach2 == reach, d2, 0.0) + jnp.where(reach3 == reach, d3, 0.0)

    def pass_on(c):
        bwd[c][0].wait_recv()
        out_d[c] = (
            d_rows[3, c, :prefix_len] + in_a[c].astype(jnp.float32)
        ).astype(jnp.bfloat16)
        bwd[c][3].start()

    def reward_copy(step):
        return pltpu.make_async_remote_copy(
            src_ref=message,
            dst_ref=table.at[my_all],
            send_sem=rew_send.at[step],
            recv_sem=rew_recv.at[step],
            device_id=place(step),
            device_id_type=MESH,
        )

    def tell(step, carry):
        reward_copy(step).start()
        return carry

    far_stats = [jnp.zeros((LAST_ROWS, HD), jnp.float32)] * 2
    for g in range(heads_kv):
        for c in (2 * g, 2 * g + 1):
            wait_arrival(c, 1 + odd, 4 * odd)
            fwd[c][0].wait_recv()
            fwd[c][3].wait_recv()
        for r in (2, 3):
            k, v = far_keys(r, g)
            reward, packed = last_token(r, g, k, v)
            note = note + jnp.where(slot_row == r, reward, 0.0)
            far_stats[r - 2] = far_stats[r - 2] + packed
        if g == heads_kv - 1:
            for r in (2, 3):
                note = note + jnp.where(
                    slot_row == slots + r - 2, offsets[0, r].astype(jnp.float32), 0.0
                )
            message[...] = note
            table[my_all] = note
            lax.fori_loop(1, n_all, tell, 0)
            sent_stats[...] = jnp.concatenate([x[:group] for x in far_stats], axis=0)
            for to in range(4):
                notes[1][to].start()
        for r in (2, 3):
            main(r, g, *far_keys(r, g))
        for chunk in (2 * g, 2 * g + 1):
            d2 = d_rows[2, chunk, :prefix_len]
            d3 = d_rows[3, chunk, :prefix_len]
            out_a[chunk] = part(d2, d3, 2 * odd - 1).astype(jnp.bfloat16)
            bwd[chunk][0].start()
            out_c[chunk] = part(d2, d3, 4 * odd - 2).astype(jnp.bfloat16)
            bwd[chunk][2].start()
            out_b[chunk] = part(d2, d3, 1 - 2 * odd).astype(jnp.bfloat16)
            bwd[chunk][1].start()
            d_rows[2, chunk, :prefix_len] = part(d2, d3, 0)
            d_rows[3, chunk, :prefix_len] = part(d2, d3, 2 - 4 * odd)
        if g > 0:
            pass_on(2 * g - 2)
            pass_on(2 * g - 1)
    pass_on(chunks - 2)
    pass_on(chunks - 1)

    def hear(step, carry):
        reward_copy(step).wait()
        return carry

    lax.fori_loop(1, n_all, hear, 0)

    summed = jnp.sum(table[...].reshape(n_dp, n_tensor, 8, HD), axis=1).reshape(n_dp * 8, HD)
    reward_sum[...] = summed
    resp = partner.shape[1]
    other = partner[...]
    label = labels[...]
    all_rows = lax.broadcasted_iota(jnp.int32, (n_dp * 8, resp), 0)
    all_ids = lax.rem(all_rows, 8) + lax.div(all_rows, 8) * slots
    all_ids = jnp.where(lax.rem(all_rows, 8) < slots, all_ids, -1)
    pair = lax.broadcasted_iota(jnp.int32, (n_dp * 8, resp), 1)
    column = summed[:, :1]
    first = jnp.sum(jnp.where(all_ids == pair, column, 0.0), axis=0, keepdims=True)
    second = jnp.sum(jnp.where(all_ids == other, column, 0.0), axis=0, keepdims=True)
    middle = 0.5 * (first + second)
    exp_first = jnp.exp(first)
    exp_second = jnp.exp(second)
    exp_middle = jnp.exp(middle)
    totals = exp_first + exp_second + exp_middle
    chosen = jnp.where(label == 0, first, jnp.where(label == 1, second, middle))
    loss = jnp.sum(jnp.log(totals) - chosen, axis=1, keepdims=True) * (1.0 / resp)
    loss_out[0] = loss[0, 0]
    tie_share = 0.5 * exp_middle / totals
    half_tie = jnp.where(label == 2, 0.5, 0.0)
    grad_first = exp_first / totals + tie_share - jnp.where(label == 0, 1.0, 0.0) - half_tie
    grad_second = exp_second / totals + tie_share - jnp.where(label == 1, 1.0, 0.0) - half_tie

    def gradient_of(ids):
        at = lax.broadcasted_iota(jnp.int32, (ids.shape[0], resp), 1)
        return jnp.sum(
            jnp.where(ids == at, grad_first, 0.0) + jnp.where(ids == other, grad_second, 0.0),
            axis=1,
            keepdims=True,
        )

    own = reward_sum[pl.ds(pl.multiple_of(me * 8, 8), 8)]
    for j in range(slots):
        rewards_out[j] = own[j, 0]

    def finish(r, g, k, v):
        mine = gradient_of(jnp.full((LAST_ROWS, resp), me * slots + r, jnp.int32))
        up31 = dot(pick, stacked(up_buf, r, g), 1, 0)
        d31 = (up31 + mine * probe_of(g)).astype(jnp.bfloat16)
        dw = dot(d31, v, 1, 1)
        delta = jnp.sum(d31.astype(jnp.float32) * o_last[r, g], axis=1, keepdims=True)
        ds = (p_last[r, g] * (dw - delta) * scale).astype(jnp.bfloat16)
        dk = d_rows[r, 2 * g, prefix_len:] + dot(ds[:, prefix_len:], q_last[r, g], 0, 0)
        dv = d_rows[r, 2 * g + 1, prefix_len:] + dot(w_last[r, g][:, prefix_len:], d31, 0, 0)
        dq = dot(pick, dot(ds, k, 1, 0).astype(jnp.bfloat16), 0, 0).astype(jnp.bfloat16)
        for h in range(group):
            cols = slice((g * group + h) * HD, (g * group + h + 1) * HD)
            gq_buf[r, :, cols] = gq_buf[r, :, cols] + dq[h * rows : (h + 1) * rows]
        mine_rows = slice(r * rows, (r + 1) * rows)
        grad_r_out[0, mine_rows, head(g)] = dk.astype(jnp.bfloat16)
        grad_r_out[1, mine_rows, head(g)] = dv.astype(jnp.bfloat16)

    for g in range(heads_kv):
        for r in range(slots):
            if r < 2:
                finish(r, g, *key_value(r, g, prefix[0, :, head(g)], prefix[1, :, head(g)]))
            else:
                finish(r, g, *far_keys(r, g))
    store_q = pltpu.make_async_copy(gq_buf, grad_q_hbm, local_sem.at[2])
    store_q.start()

    near_by = (0, 0, -1, 1, -2, 2)
    pair_rows = lax.broadcasted_iota(jnp.int32, (2 * group, resp), 0)
    second_slot = pair_rows >= group
    grad_rows = []
    used = []
    for i, reach in enumerate(near_by):
        device = lax.rem(me + n_dp + reach, n_dp)
        first_slot = 0 if i == 0 else 2
        ids = jnp.where(second_slot, 1, 0) + (device * slots + first_slot)
        grad_rows.append(gradient_of(ids))
        if i == 0:
            used.append(jnp.ones((2 * group, 1), jnp.float32))
        else:
            told = table[device * n_tensor]
            offset = jnp.where(
                second_slot[:, :1], told[slots + 1 : slots + 2, :1], told[slots : slots + 1, :1]
            )
            used.append(jnp.where(offset == float(-reach), 1.0, 0.0))
    grad_rows = jnp.concatenate(grad_rows, axis=0)
    used = jnp.concatenate(used, axis=0)
    for which in range(2):
        for to in range(4):
            notes[which][to].wait_recv()
    stats = jnp.concatenate(
        [stats_near[...], sent_stats[...]] + [got_stats[to] for to in range(4)], axis=0
    )
    for g in range(heads_kv):
        q31 = jnp.concatenate(
            [jnp.concatenate([q_last[0, g][:group], q_last[1, g][:group]], axis=0), sent_rows[0, g]]
            + [got_rows[to, 0, g] for to in range(4)],
            axis=0,
        )
        near_up = [dot(pick, stacked(up_buf, r, g), 1, 0)[:group] for r in (0, 1)]
        up31 = jnp.concatenate(
            near_up
            + [sent_rows[1, g].astype(jnp.float32)]
            + [got_rows[to, 1, g].astype(jnp.float32) for to in range(4)],
            axis=0,
        )
        probes = jnp.concatenate([probe[g * group : (g + 1) * group]] * (2 * len(near_by)), axis=0)
        top, inverse, up_o, probe_o = [stats[:, 4 * g + i : 4 * g + i + 1] for i in range(4)]
        k, v = prefix[0, :, head(g)], prefix[1, :, head(g)]
        d31 = (up31 + grad_rows * probes).astype(jnp.bfloat16)
        w = jnp.where(used > 0.0, jnp.exp((dot(q31, k, 1, 1) - top) * scale) * inverse, 0.0)
        dw = dot(d31, v, 1, 1)
        ds = (w * (dw - (up_o + grad_rows * probe_o)) * scale).astype(jnp.bfloat16)
        d_rows[2, 2 * g, :prefix_len] += (
            d_rows[0, 2 * g, :prefix_len] + d_rows[1, 2 * g, :prefix_len] + dot(ds, q31, 0, 0)
        )
        d_rows[2, 2 * g + 1, :prefix_len] += (
            d_rows[0, 2 * g + 1, :prefix_len]
            + d_rows[1, 2 * g + 1, :prefix_len]
            + dot(w.astype(jnp.bfloat16), d31, 0, 0)
        )

    for c in range(chunks):
        bwd[c][1].wait_recv()
        bwd[c][2].wait_recv()
        bwd[c][3].wait_recv()
        grad_p_out[c % 2, :, head(c // 2)] = (
            d_rows[2, c, :prefix_len]
            + in_b[c].astype(jnp.float32)
            + in_c[c].astype(jnp.float32)
            + in_d[c].astype(jnp.float32)
        ).astype(jnp.bfloat16)

    for c in range(chunks):
        for k in range(4):
            fwd[c][k].wait_send()
            bwd[c][k].wait_send()
    for which in range(2):
        for to in range(4):
            notes[which][to].wait_send()
    store_q.wait()


def per_device(
    n_dp,
    n_tensor,
    queries,
    response_cache,
    prefix_cache,
    upstream,
    reward_probe,
    slot_offsets,
    partner,
    labels,
):
    slots, rows, width = queries.shape
    prefix_len = prefix_cache.shape[1]
    kv_heads = response_cache.shape[3] // HD
    chunks = 2 * kv_heads
    keys = prefix_len + rows
    group = width // HD // kv_heads
    resp = partner.shape[0]
    n_all = n_dp * n_tensor
    kv_width = kv_heads * HD
    prefix = prefix_cache[0].transpose(1, 0, 2)
    response = response_cache.reshape(slots * rows, 2, kv_width).transpose(1, 0, 2)
    vmem = pl.BlockSpec(memory_space=pltpu.VMEM)
    smem = pl.BlockSpec(memory_space=pltpu.SMEM)
    hbm = pl.BlockSpec(memory_space=pl.ANY)
    near = pltpu.VMEM((2 * SPAN + 1, prefix_len, HD), jnp.bfloat16)
    block = pltpu.VMEM((chunks, prefix_len, HD), jnp.bfloat16)
    rewards, loss, grad_q, grad_r, grad_p = pl.pallas_call(
        functools.partial(kernel, n_dp, n_tensor),
        out_shape=(
            jax.ShapeDtypeStruct((slots,), jnp.float32),
            jax.ShapeDtypeStruct((1,), jnp.float32),
            jax.ShapeDtypeStruct(queries.shape, jnp.bfloat16),
            jax.ShapeDtypeStruct((2, slots * rows, kv_width), jnp.bfloat16),
            jax.ShapeDtypeStruct((2, prefix_len, kv_width), jnp.bfloat16),
        ),
        in_specs=[smem, hbm, hbm, vmem, vmem, vmem, vmem, vmem],
        out_specs=(smem, smem, hbm, vmem, vmem),
        scratch_shapes=[
            pltpu.VMEM(queries.shape, jnp.bfloat16),
            pltpu.VMEM(queries.shape, jnp.bfloat16),
            pltpu.VMEM(queries.shape, jnp.bfloat16),
            near,
            near,
            near,
            near,
            pltpu.VMEM((slots, chunks, keys, HD), jnp.float32),
            pltpu.VMEM((slots, kv_heads, LAST_ROWS, keys), jnp.bfloat16),
            pltpu.VMEM((slots, kv_heads, LAST_ROWS, keys), jnp.float32),
            pltpu.VMEM((slots, kv_heads, LAST_ROWS, HD), jnp.float32),
            pltpu.VMEM((slots, kv_heads, LAST_ROWS, HD), jnp.bfloat16),
            pltpu.VMEM((8, HD), jnp.float32),
            pltpu.VMEM((n_all, 8, HD), jnp.float32),
            pltpu.VMEM((n_dp * 8, HD), jnp.float32),
            pltpu.VMEM((2, kv_heads, 2 * group, HD), jnp.bfloat16),
            pltpu.VMEM((4, 2, kv_heads, 2 * group, HD), jnp.bfloat16),
            pltpu.VMEM((2 * group, HD), jnp.float32),
            pltpu.VMEM((4, 2 * group, HD), jnp.float32),
            pltpu.VMEM((2 * group, HD), jnp.float32),
            block,
            block,
            block,
            block,
            block,
            block,
            block,
            block,
            pltpu.SemaphoreType.DMA((3,)),
            pltpu.SemaphoreType.DMA((chunks, 4)),
            pltpu.SemaphoreType.DMA((chunks, 4)),
            pltpu.SemaphoreType.DMA((chunks, 4)),
            pltpu.SemaphoreType.DMA((chunks, 4)),
            pltpu.SemaphoreType.DMA((n_all,)),
            pltpu.SemaphoreType.DMA((n_all,)),
            pltpu.SemaphoreType.DMA((2, 4)),
            pltpu.SemaphoreType.DMA((2, 4)),
        ],
        compiler_params=pltpu.CompilerParams(
            collective_id=0, has_side_effects=True, vmem_limit_bytes=40 * 1024 * 1024
        ),
    )(
        slot_offsets,
        queries,
        upstream,
        prefix,
        response,
        reward_probe.reshape(width // HD, HD),
        partner.reshape(1, resp),
        labels.reshape(1, resp),
    )
    grad_response = grad_r.transpose(1, 0, 2)
    grad_prefix = grad_p.transpose(1, 0, 2)
    return (
        rewards,
        loss,
        grad_q,
        grad_response.reshape(response_cache.shape),
        grad_prefix.reshape(prefix_cache.shape),
    )


def solution(mesh):
    in_specs = (
        P(("group", "dp"), None, "tensor"),
        P(("group", "dp"), None, None, "tensor"),
        P(("group", "dp"), None, None, "tensor"),
        P(("group", "dp"), None, "tensor"),
        P("tensor"),
        P(("group", "dp"), None),
        P("group"),
        P("group"),
    )
    out_specs = (
        P(("group", "dp")),
        P("group"),
        P(("group", "dp"), None, "tensor"),
        P(("group", "dp"), None, None, "tensor"),
        P(("group", "dp"), None, None, "tensor"),
    )
    return jax.shard_map(
        functools.partial(per_device, mesh.shape["dp"], mesh.shape["tensor"]),
        mesh=mesh,
        in_specs=in_specs,
        out_specs=out_specs,
        check_vma=False,
    )
```

```python
import functools
import math

import jax
import jax.numpy as jnp
from jax import lax
from jax.experimental import pallas as pl
from jax.experimental.pallas import tpu as pltpu
from jax.sharding import PartitionSpec as P

HD = 128
SPAN = 2
LAST_ROWS = 16
MESH = pl.DeviceIdType.MESH


def dot(a, b, contract_a, contract_b):
    return lax.dot_general(
        a, b, (((contract_a,), (contract_b,)), ((), ())), preferred_element_type=jnp.float32
    )


def kernel(
    n_dp,
    n_tensor,
    offsets_hbm,
    queries_hbm,
    upstream_hbm,
    prefix_hbm,
    response_hbm,
    probe_hbm,
    partner_hbm,
    labels_hbm,
    rewards_out,
    loss_out,
    grad_q_hbm,
    grad_r_out,
    grad_p_out,
    prefix_raw,
    response_raw,
    probe,
    partner,
    labels,
    offsets,
    prefix,
    response,
    grad_r,
    q_buf,
    up_buf,
    gq_buf,
    near0,
    near1,
    near2,
    near3,
    d_rows,
    w_last,
    p_last,
    o_last,
    q_last,
    message,
    table,
    reward_sum,
    sent_rows,
    got_rows,
    sent_stats,
    got_stats,
    stats_near,
    out_a,
    out_b,
    out_c,
    out_d,
    in_a,
    in_b,
    in_c,
    in_d,
    local_sem,
    fwd_send,
    fwd_recv,
    bwd_send,
    bwd_recv,
    rew_send,
    rew_recv,
    note_send,
    note_recv,
):
    slots, rows, width = q_buf.shape
    _, prefix_len, kv_width = prefix.shape
    heads_kv = kv_width // HD
    chunks = 2 * heads_kv
    group = width // HD // heads_kv
    keys = prefix_len + rows
    m_len = group * rows
    near = (near0, near1, near2, near3)
    scale = 1.0 / math.sqrt(HD)

    me = lax.axis_index("dp")
    my_t = lax.axis_index("tensor")
    odd = lax.rem(me, 2)
    mate = me + 1 - 2 * odd
    soon = lax.rem(me + n_dp - 2 + 4 * odd, n_dp)
    later = lax.rem(me + n_dp + 2 - 4 * odd, n_dp)
    n_all = n_dp * n_tensor
    my_all = me * n_tensor + my_t

    def place(step):
        other = lax.rem(my_all + step, n_all)
        return {"dp": lax.div(other, n_tensor), "tensor": lax.rem(other, n_tensor)}

    loads = [
        pltpu.make_async_copy(src, dst, local_sem.at[3 + i])
        for i, (src, dst) in enumerate(
            (
                (prefix_hbm, prefix_raw),
                (response_hbm, response_raw),
                (probe_hbm, probe),
                (offsets_hbm, offsets),
                (partner_hbm, partner),
                (labels_hbm, labels),
            )
        )
    ]
    for load in loads:
        load.start()
    load_q = pltpu.make_async_copy(queries_hbm, q_buf, local_sem.at[0])
    load_up = pltpu.make_async_copy(upstream_hbm, up_buf, local_sem.at[1])
    load_q.start()
    load_up.start()

    barrier = pltpu.get_barrier_semaphore()

    def greet(step, carry):
        pl.semaphore_signal(barrier, inc=1, device_id=place(step), device_id_type=MESH)
        return carry

    lax.fori_loop(1, n_all, greet, 0)
    loads[0].wait()
    prefix[...] = jnp.swapaxes(prefix_raw[0], 0, 1)
    pl.semaphore_wait(barrier, n_all - 1)

    def head(g):
        return slice(g * HD, (g + 1) * HD)

    def prefix_at(chunk):
        return prefix.at[chunk % 2, :, head(chunk // 2)]

    def forward_copy(chunk, kind):
        if kind == 0:
            src, dst, to = prefix_at(chunk), near[chunk].at[1 + 2 * odd], mate
        elif kind == 1:
            src, dst, to = prefix_at(chunk), near[chunk].at[4 - 4 * odd], soon
        elif kind == 2:
            src, dst, to = prefix_at(chunk), near[chunk].at[4 * odd], later
        else:
            src, dst, to = near[chunk].at[4 - 4 * odd], near[chunk].at[3 - 2 * odd], mate
        return pltpu.make_async_remote_copy(
            src_ref=src,
            dst_ref=dst,
            send_sem=fwd_send.at[chunk, kind],
            recv_sem=fwd_recv.at[chunk, kind],
            device_id={"dp": to},
            device_id_type=MESH,
        )

    fwd = [[forward_copy(c, k) for k in range(4)] for c in range(chunks)]
    for k in (1, 0, 2):
        for c in range(chunks):
            fwd[c][k].start()

    lane = lax.broadcasted_iota(jnp.int32, (1, m_len), 1)
    token = lax.rem(lane, rows)
    not_last = jnp.where(token == rows - 1, 0.0, 1.0)
    causal = lax.broadcasted_iota(jnp.int32, (rows, m_len), 0) <= lax.rem(
        lax.broadcasted_iota(jnp.int32, (rows, m_len), 1), rows
    )
    pick = jnp.where(
        lax.broadcasted_iota(jnp.int32, (LAST_ROWS, m_len), 0) * rows + (rows - 1)
        == lax.broadcasted_iota(jnp.int32, (LAST_ROWS, m_len), 1),
        1.0,
        0.0,
    ).astype(jnp.bfloat16)

    def stacked(buf, r, g):
        return jnp.concatenate(
            [buf[r, :, (g * group + h) * HD : (g * group + h + 1) * HD] for h in range(group)],
            axis=0,
        )

    def key_value(r, g, prefix_k, prefix_v):
        mine = pl.ds(pl.multiple_of(r * rows, rows), rows)
        return (
            jnp.concatenate([prefix_k, response[0, mine, head(g)]], axis=0),
            jnp.concatenate([prefix_v, response[1, mine, head(g)]], axis=0),
        )

    def probe_of(g):
        return jnp.concatenate(
            [probe[g * group : (g + 1) * group], jnp.zeros((LAST_ROWS - group, HD), jnp.float32)],
            axis=0,
        )

    def last_token(r, g, k, v):
        q31 = dot(pick, stacked(q_buf, r, g), 1, 0).astype(jnp.bfloat16)
        s = dot(q31, k, 1, 1)
        e = jnp.exp((s - jnp.max(s, axis=1, keepdims=True)) * scale)
        w = e / jnp.sum(e, axis=1, keepdims=True)
        w_low = w.astype(jnp.bfloat16)
        o = dot(w_low, v, 1, 0)
        q_last[r, g] = q31
        w_last[r, g] = w_low
        p_last[r, g] = w
        o_last[r, g] = o
        by_head = jnp.sum(o * probe_of(g), axis=1, keepdims=True)
        stats = [
            jnp.max(s, axis=1, keepdims=True),
            1.0 / jnp.sum(e, axis=1, keepdims=True),
            jnp.sum(o * dot(pick, stacked(up_buf, r, g), 1, 0), axis=1, keepdims=True),
            by_head,
        ]
        packed = jnp.zeros((LAST_ROWS, HD), jnp.float32)
        for i, stat in enumerate(stats):
            packed = packed + jnp.where(lane_of == g * len(stats) + i, stat, 0.0)
        return jnp.sum(by_head, axis=0, keepdims=True), packed

    def main(r, g, k, v):
        q = stacked(q_buf, r, g)
        d_out = stacked(up_buf, r, g)
        s = dot(k, q, 1, 1)
        s = jnp.concatenate(
            [s[:prefix_len], jnp.where(causal, s[prefix_len:], -1e30)], axis=0
        )
        e = jnp.exp((s - jnp.max(s, axis=0, keepdims=True)) * scale)
        w = e * (not_last / jnp.sum(e, axis=0, keepdims=True))
        w_low = w.astype(jnp.bfloat16)
        dw = dot(v, d_out, 1, 1)
        delta = jnp.sum(w_low.astype(jnp.float32) * dw, axis=0, keepdims=True)
        ds = (w * (dw - delta) * scale).astype(jnp.bfloat16)
        d_rows[r, 2 * g] = dot(ds, q, 1, 0)
        d_rows[r, 2 * g + 1] = dot(w_low, d_out, 1, 0)
        dq = dot(ds, k, 0, 0).astype(jnp.bfloat16)
        for h in range(group):
            gq_buf[r, :, (g * group + h) * HD : (g * group + h + 1) * HD] = dq[
                h * rows : (h + 1) * rows
            ]

    slot_row = lax.broadcasted_iota(jnp.int32, (8, HD), 0)
    lane_of = lax.broadcasted_iota(jnp.int32, (LAST_ROWS, HD), 1)

    for load in loads[1:]:
        load.wait()
    response[...] = jnp.swapaxes(
        response_raw[...].reshape(slots * rows, 2, kv_width), 0, 1
    )
    load_q.wait()
    load_up.wait()

    for g in range(heads_kv):
        for i, buf in enumerate((q_buf, up_buf)):
            both = [dot(pick, stacked(buf, r, g), 1, 0)[:group] for r in (2, 3)]
            sent_rows[i, g] = jnp.concatenate(both, axis=0).astype(jnp.bfloat16)

    def note_copy(which, to):
        src = (sent_rows, sent_stats)[which]
        dst = (got_rows, got_stats)[which].at[to]
        near_by = (1, n_dp - 1, 2, n_dp - 2)[to]
        return pltpu.make_async_remote_copy(
            src_ref=src,
            dst_ref=dst,
            send_sem=note_send.at[which, to],
            recv_sem=note_recv.at[which, to],
            device_id={"dp": lax.rem(me + near_by, n_dp)},
            device_id_type=MESH,
        )

    notes = [[note_copy(which, to) for to in range(4)] for which in range(2)]

    for c in range(chunks):
        near[c][2] = prefix[c % 2, :, head(c // 2)]
    note = jnp.zeros((8, HD), jnp.float32)
    own_stats = []
    for r in (0, 1):
        mine = jnp.zeros((LAST_ROWS, HD), jnp.float32)
        for g in range(heads_kv):
            k, v = key_value(r, g, prefix[0, :, head(g)], prefix[1, :, head(g)])
            reward, packed = last_token(r, g, k, v)
            note = note + jnp.where(slot_row == r, reward, 0.0)
            mine = mine + packed
            main(r, g, k, v)
        own_stats.append(mine[:group])
        for c in (2 * r, 2 * r + 1):
            fwd[c][1].wait_recv()
            fwd[c][3].start()
    stats_near[...] = jnp.concatenate(own_stats, axis=0)

    for to in range(4):
        notes[0][to].start()

    def backward_copy(chunk, kind):
        src = (out_a, out_b, out_c, out_d)[kind].at[chunk]
        dst = (in_a, in_b, in_c, in_d)[kind].at[chunk]
        if kind < 2:
            to = mate
        elif kind == 2:
            to = soon
        else:
            to = later
        return pltpu.make_async_remote_copy(
            src_ref=src,
            dst_ref=dst,
            send_sem=bwd_send.at[chunk, kind],
            recv_sem=bwd_recv.at[chunk, kind],
            device_id={"dp": to},
            device_id_type=MESH,
        )

    bwd = [[backward_copy(c, k) for k in range(4)] for c in range(chunks)]
    reach2 = offsets[0, 2]
    reach3 = offsets[0, 3]

    def far_keys(r, g):
        reach = offsets[0, r] + SPAN
        return key_value(r, g, near[2 * g][reach], near[2 * g + 1][reach])

    def part(d2, d3, reach):
        return jnp.where(reach2 == reach, d2, 0.0) + jnp.where(reach3 == reach, d3, 0.0)

    def pass_on(c):
        bwd[c][0].wait_recv()
        out_d[c] = (
            d_rows[3, c, :prefix_len] + in_a[c].astype(jnp.float32)
        ).astype(jnp.bfloat16)
        bwd[c][3].start()

    def reward_copy(step):
        return pltpu.make_async_remote_copy(
            src_ref=message,
            dst_ref=table.at[my_all],
            send_sem=rew_send.at[step],
            recv_sem=rew_recv.at[step],
            device_id=place(step),
            device_id_type=MESH,
        )

    def tell(step, carry):
        reward_copy(step).start()
        return carry

    far_stats = [jnp.zeros((LAST_ROWS, HD), jnp.float32)] * 2
    for g in range(heads_kv):
        for c in (2 * g, 2 * g + 1):
            fwd[c][2].wait_recv()
            fwd[c][0].wait_recv()
            fwd[c][3].wait_recv()
        for r in (2, 3):
            k, v = far_keys(r, g)
            reward, packed = last_token(r, g, k, v)
            note = note + jnp.where(slot_row == r, reward, 0.0)
            far_stats[r - 2] = far_stats[r - 2] + packed
        if g == heads_kv - 1:
            for r in (2, 3):
                note = note + jnp.where(
                    slot_row == slots + r - 2, offsets[0, r].astype(jnp.float32), 0.0
                )
            message[...] = note
            table[my_all] = note
            lax.fori_loop(1, n_all, tell, 0)
            sent_stats[...] = jnp.concatenate([x[:group] for x in far_stats], axis=0)
            for to in range(4):
                notes[1][to].start()
        for r in (2, 3):
            main(r, g, *far_keys(r, g))
        for chunk in (2 * g, 2 * g + 1):
            d2 = d_rows[2, chunk, :prefix_len]
            d3 = d_rows[3, chunk, :prefix_len]
            out_a[chunk] = part(d2, d3, 2 * odd - 1).astype(jnp.bfloat16)
            bwd[chunk][0].start()
            out_c[chunk] = part(d2, d3, 4 * odd - 2).astype(jnp.bfloat16)
            bwd[chunk][2].start()
            out_b[chunk] = part(d2, d3, 1 - 2 * odd).astype(jnp.bfloat16)
            d_rows[2, chunk, :prefix_len] = part(d2, d3, 0)
            d_rows[3, chunk, :prefix_len] = part(d2, d3, 2 - 4 * odd)
    for c in range(chunks):
        pass_on(c)
    for c in range(chunks):
        bwd[c][0].wait_send()
        bwd[c][1].start()

    def hear(step, carry):
        reward_copy(step).wait()
        return carry

    lax.fori_loop(1, n_all, hear, 0)

    summed = jnp.sum(table[...].reshape(n_dp, n_tensor, 8, HD), axis=1).reshape(n_dp * 8, HD)
    reward_sum[...] = summed
    resp = partner.shape[1]
    other = partner[...]
    label = labels[...]
    all_rows = lax.broadcasted_iota(jnp.int32, (n_dp * 8, resp), 0)
    all_ids = lax.rem(all_rows, 8) + lax.div(all_rows, 8) * slots
    all_ids = jnp.where(lax.rem(all_rows, 8) < slots, all_ids, -1)
    pair = lax.broadcasted_iota(jnp.int32, (n_dp * 8, resp), 1)
    column = summed[:, :1]
    first = jnp.sum(jnp.where(all_ids == pair, column, 0.0), axis=0, keepdims=True)
    second = jnp.sum(jnp.where(all_ids == other, column, 0.0), axis=0, keepdims=True)
    middle = 0.5 * (first + second)
    exp_first = jnp.exp(first)
    exp_second = jnp.exp(second)
    exp_middle = jnp.exp(middle)
    totals = exp_first + exp_second + exp_middle
    chosen = jnp.where(label == 0, first, jnp.where(label == 1, second, middle))
    loss = jnp.sum(jnp.log(totals) - chosen, axis=1, keepdims=True) * (1.0 / resp)
    loss_out[0] = loss[0, 0]
    tie_share = 0.5 * exp_middle / totals
    half_tie = jnp.where(label == 2, 0.5, 0.0)
    grad_first = exp_first / totals + tie_share - jnp.where(label == 0, 1.0, 0.0) - half_tie
    grad_second = exp_second / totals + tie_share - jnp.where(label == 1, 1.0, 0.0) - half_tie

    def gradient_of(ids):
        at = lax.broadcasted_iota(jnp.int32, (ids.shape[0], resp), 1)
        return jnp.sum(
            jnp.where(ids == at, grad_first, 0.0) + jnp.where(ids == other, grad_second, 0.0),
            axis=1,
            keepdims=True,
        )

    own = reward_sum[pl.ds(pl.multiple_of(me * 8, 8), 8)]
    for j in range(slots):
        rewards_out[j] = own[j, 0]

    def finish(r, g, k, v):
        mine = gradient_of(jnp.full((LAST_ROWS, resp), me * slots + r, jnp.int32))
        up31 = dot(pick, stacked(up_buf, r, g), 1, 0)
        d31 = (up31 + mine * probe_of(g)).astype(jnp.bfloat16)
        dw = dot(d31, v, 1, 1)
        delta = jnp.sum(d31.astype(jnp.float32) * o_last[r, g], axis=1, keepdims=True)
        ds = (p_last[r, g] * (dw - delta) * scale).astype(jnp.bfloat16)
        dk = d_rows[r, 2 * g, prefix_len:] + dot(ds[:, prefix_len:], q_last[r, g], 0, 0)
        dv = d_rows[r, 2 * g + 1, prefix_len:] + dot(w_last[r, g][:, prefix_len:], d31, 0, 0)
        dq = dot(pick, dot(ds, k, 1, 0).astype(jnp.bfloat16), 0, 0).astype(jnp.bfloat16)
        for h in range(group):
            cols = slice((g * group + h) * HD, (g * group + h + 1) * HD)
            gq_buf[r, :, cols] = gq_buf[r, :, cols] + dq[h * rows : (h + 1) * rows]
        mine_rows = slice(r * rows, (r + 1) * rows)
        grad_r[0, mine_rows, head(g)] = dk.astype(jnp.bfloat16)
        grad_r[1, mine_rows, head(g)] = dv.astype(jnp.bfloat16)

    for g in range(heads_kv):
        for r in range(slots):
            if r < 2:
                finish(r, g, *key_value(r, g, prefix[0, :, head(g)], prefix[1, :, head(g)]))
            else:
                finish(r, g, *far_keys(r, g))
    grad_r_out[...] = jnp.swapaxes(grad_r[...], 0, 1).reshape(grad_r_out.shape)
    store_q = pltpu.make_async_copy(gq_buf, grad_q_hbm, local_sem.at[2])
    store_q.start()

    near_by = (0, 0, -1, 1, -2, 2)
    pair_rows = lax.broadcasted_iota(jnp.int32, (2 * group, resp), 0)
    second_slot = pair_rows >= group
    grad_rows = []
    used = []
    for i, reach in enumerate(near_by):
        device = lax.rem(me + n_dp + reach, n_dp)
        first_slot = 0 if i == 0 else 2
        ids = jnp.where(second_slot, 1, 0) + (device * slots + first_slot)
        grad_rows.append(gradient_of(ids))
        if i == 0:
            used.append(jnp.ones((2 * group, 1), jnp.float32))
        else:
            told = table[device * n_tensor]
            offset = jnp.where(
                second_slot[:, :1], told[slots + 1 : slots + 2, :1], told[slots : slots + 1, :1]
            )
            used.append(jnp.where(offset == float(-reach), 1.0, 0.0))
    grad_rows = jnp.concatenate(grad_rows, axis=0)
    used = jnp.concatenate(used, axis=0)
    for which in range(2):
        for to in range(4):
            notes[which][to].wait_recv()
    stats = jnp.concatenate(
        [stats_near[...], sent_stats[...]] + [got_stats[to] for to in range(4)], axis=0
    )
    for g in range(heads_kv):
        q31 = jnp.concatenate(
            [jnp.concatenate([q_last[0, g][:group], q_last[1, g][:group]], axis=0), sent_rows[0, g]]
            + [got_rows[to, 0, g] for to in range(4)],
            axis=0,
        )
        near_up = [dot(pick, stacked(up_buf, r, g), 1, 0)[:group] for r in (0, 1)]
        up31 = jnp.concatenate(
            near_up
            + [sent_rows[1, g].astype(jnp.float32)]
            + [got_rows[to, 1, g].astype(jnp.float32) for to in range(4)],
            axis=0,
        )
        probes = jnp.concatenate([probe[g * group : (g + 1) * group]] * (2 * len(near_by)), axis=0)
        top, inverse, up_o, probe_o = [stats[:, 4 * g + i : 4 * g + i + 1] for i in range(4)]
        k, v = prefix[0, :, head(g)], prefix[1, :, head(g)]
        d31 = (up31 + grad_rows * probes).astype(jnp.bfloat16)
        w = jnp.where(used > 0.0, jnp.exp((dot(q31, k, 1, 1) - top) * scale) * inverse, 0.0)
        dw = dot(d31, v, 1, 1)
        ds = (w * (dw - (up_o + grad_rows * probe_o)) * scale).astype(jnp.bfloat16)
        d_rows[2, 2 * g, :prefix_len] += (
            d_rows[0, 2 * g, :prefix_len] + d_rows[1, 2 * g, :prefix_len] + dot(ds, q31, 0, 0)
        )
        d_rows[2, 2 * g + 1, :prefix_len] += (
            d_rows[0, 2 * g + 1, :prefix_len]
            + d_rows[1, 2 * g + 1, :prefix_len]
            + dot(w.astype(jnp.bfloat16), d31, 0, 0)
        )

    for c in range(chunks):
        for k in range(4):
            fwd[c][k].wait_send()
    for c in range(chunks):
        bwd[c][1].wait_recv()
        bwd[c][2].wait_recv()
        bwd[c][3].wait_recv()
        prefix[c % 2, :, head(c // 2)] = (
            d_rows[2, c, :prefix_len]
            + in_b[c].astype(jnp.float32)
            + in_c[c].astype(jnp.float32)
            + in_d[c].astype(jnp.float32)
        ).astype(jnp.bfloat16)

    for c in range(chunks):
        for k in (1, 2, 3):
            bwd[c][k].wait_send()
    grad_p_out[...] = jnp.swapaxes(prefix[...], 0, 1)[None]
    for which in range(2):
        for to in range(4):
            notes[which][to].wait_send()
    store_q.wait()


def per_device(
    n_dp,
    n_tensor,
    queries,
    response_cache,
    prefix_cache,
    upstream,
    reward_probe,
    slot_offsets,
    partner,
    labels,
):
    slots, rows, width = queries.shape
    prefix_len = prefix_cache.shape[1]
    kv_heads = response_cache.shape[3] // HD
    chunks = 2 * kv_heads
    keys = prefix_len + rows
    group = width // HD // kv_heads
    resp = partner.shape[0]
    n_all = n_dp * n_tensor
    kv_width = kv_heads * HD
    kv_width = kv_heads * HD
    vmem = pl.BlockSpec(memory_space=pltpu.VMEM)
    smem = pl.BlockSpec(memory_space=pltpu.SMEM)
    hbm = pl.BlockSpec(memory_space=pl.ANY)
    near = pltpu.VMEM((2 * SPAN + 1, prefix_len, HD), jnp.bfloat16)
    block = pltpu.VMEM((chunks, prefix_len, HD), jnp.bfloat16)
    rewards, loss, grad_q, grad_r, grad_p = pl.pallas_call(
        functools.partial(kernel, n_dp, n_tensor),
        out_shape=(
            jax.ShapeDtypeStruct((slots,), jnp.float32),
            jax.ShapeDtypeStruct((1,), jnp.float32),
            jax.ShapeDtypeStruct(queries.shape, jnp.bfloat16),
            jax.ShapeDtypeStruct(response_cache.shape, jnp.bfloat16),
            jax.ShapeDtypeStruct(prefix_cache.shape, jnp.bfloat16),
        ),
        in_specs=[hbm] * 8,
        out_specs=(smem, smem, hbm, vmem, vmem),
        scratch_shapes=[
            pltpu.VMEM(prefix_cache.shape, jnp.bfloat16),
            pltpu.VMEM(response_cache.shape, jnp.bfloat16),
            pltpu.VMEM((width // HD, HD), jnp.float32),
            pltpu.VMEM((1, resp), jnp.int32),
            pltpu.VMEM((1, resp), jnp.int32),
            pltpu.SMEM((1, slots), jnp.int32),
            pltpu.VMEM((2, prefix_len, kv_width), jnp.bfloat16),
            pltpu.VMEM((2, slots * rows, kv_width), jnp.bfloat16),
            pltpu.VMEM((2, slots * rows, kv_width), jnp.bfloat16),
            pltpu.VMEM(queries.shape, jnp.bfloat16),
            pltpu.VMEM(queries.shape, jnp.bfloat16),
            pltpu.VMEM(queries.shape, jnp.bfloat16),
            near,
            near,
            near,
            near,
            pltpu.VMEM((slots, chunks, keys, HD), jnp.float32),
            pltpu.VMEM((slots, kv_heads, LAST_ROWS, keys), jnp.bfloat16),
            pltpu.VMEM((slots, kv_heads, LAST_ROWS, keys), jnp.float32),
            pltpu.VMEM((slots, kv_heads, LAST_ROWS, HD), jnp.float32),
            pltpu.VMEM((slots, kv_heads, LAST_ROWS, HD), jnp.bfloat16),
            pltpu.VMEM((8, HD), jnp.float32),
            pltpu.VMEM((n_all, 8, HD), jnp.float32),
            pltpu.VMEM((n_dp * 8, HD), jnp.float32),
            pltpu.VMEM((2, kv_heads, 2 * group, HD), jnp.bfloat16),
            pltpu.VMEM((4, 2, kv_heads, 2 * group, HD), jnp.bfloat16),
            pltpu.VMEM((2 * group, HD), jnp.float32),
            pltpu.VMEM((4, 2 * group, HD), jnp.float32),
            pltpu.VMEM((2 * group, HD), jnp.float32),
            block,
            block,
            block,
            block,
            block,
            block,
            block,
            block,
            pltpu.SemaphoreType.DMA((9,)),
            pltpu.SemaphoreType.DMA((chunks, 4)),
            pltpu.SemaphoreType.DMA((chunks, 4)),
            pltpu.SemaphoreType.DMA((chunks, 4)),
            pltpu.SemaphoreType.DMA((chunks, 4)),
            pltpu.SemaphoreType.DMA((n_all,)),
            pltpu.SemaphoreType.DMA((n_all,)),
            pltpu.SemaphoreType.DMA((2, 4)),
            pltpu.SemaphoreType.DMA((2, 4)),
        ],
        compiler_params=pltpu.CompilerParams(
            collective_id=0, has_side_effects=True, vmem_limit_bytes=60 * 1024 * 1024
        ),
    )(
        slot_offsets,
        queries,
        upstream,
        prefix_cache,
        response_cache,
        reward_probe.reshape(width // HD, HD),
        partner.reshape(1, resp),
        labels.reshape(1, resp),
    )
    return rewards, loss, grad_q, grad_r, grad_p


def solution(mesh):
    in_specs = (
        P(("group", "dp"), None, "tensor"),
        P(("group", "dp"), None, None, "tensor"),
        P(("group", "dp"), None, None, "tensor"),
        P(("group", "dp"), None, "tensor"),
        P("tensor"),
        P(("group", "dp"), None),
        P("group"),
        P("group"),
    )
    out_specs = (
        P(("group", "dp")),
        P("group"),
        P(("group", "dp"), None, "tensor"),
        P(("group", "dp"), None, None, "tensor"),
        P(("group", "dp"), None, None, "tensor"),
    )
    return jax.shard_map(
        functools.partial(per_device, mesh.shape["dp"], mesh.shape["tensor"]),
        mesh=mesh,
        in_specs=in_specs,
        out_specs=out_specs,
        check_vma=False,
    )
```

```python
import functools
import math

import jax
import jax.numpy as jnp
from jax import lax
from jax.experimental import pallas as pl
from jax.experimental.pallas import tpu as pltpu
from jax.sharding import PartitionSpec as P

HD = 128
SPAN = 2
LAST_ROWS = 16
MESH = pl.DeviceIdType.MESH


def dot(a, b, contract_a, contract_b):
    return lax.dot_general(
        a, b, (((contract_a,), (contract_b,)), ((), ())), preferred_element_type=jnp.float32
    )


def kernel(
    n_dp,
    n_tensor,
    offsets_hbm,
    queries_hbm,
    upstream_hbm,
    prefix_hbm,
    response_hbm,
    probe_hbm,
    partner_hbm,
    labels_hbm,
    rewards_out,
    loss_out,
    grad_q_hbm,
    grad_r_out,
    grad_p_out,
    prefix_raw,
    response_raw,
    probe,
    partner,
    labels,
    offsets,
    prefix,
    response,
    grad_r,
    q_buf,
    up_buf,
    gq_buf,
    near0,
    near1,
    near2,
    near3,
    d_rows,
    w_last,
    p_last,
    o_last,
    q_last,
    message,
    table,
    reward_sum,
    sent_rows,
    got_rows,
    sent_stats,
    got_stats,
    stats_near,
    out_a,
    out_b,
    out_c,
    out_d,
    in_a,
    in_b,
    in_c,
    in_d,
    local_sem,
    fwd_send,
    fwd_recv,
    bwd_send,
    bwd_recv,
    rew_send,
    rew_recv,
    note_send,
    note_recv,
):
    slots, rows, width = q_buf.shape
    _, prefix_len, kv_width = prefix.shape
    heads_kv = kv_width // HD
    chunks = 2 * heads_kv
    group = width // HD // heads_kv
    keys = prefix_len + rows
    m_len = group * rows
    near = (near0, near1, near2, near3)
    scale = 1.0 / math.sqrt(HD)

    me = lax.axis_index("dp")
    my_t = lax.axis_index("tensor")
    odd = lax.rem(me, 2)
    mate = me + 1 - 2 * odd
    soon = lax.rem(me + n_dp - 2 + 4 * odd, n_dp)
    later = lax.rem(me + n_dp + 2 - 4 * odd, n_dp)
    n_all = n_dp * n_tensor
    my_all = me * n_tensor + my_t

    def place(step):
        other = lax.rem(my_all + step, n_all)
        return {"dp": lax.div(other, n_tensor), "tensor": lax.rem(other, n_tensor)}

    loads = [
        pltpu.make_async_copy(src, dst, local_sem.at[3 + i])
        for i, (src, dst) in enumerate(
            (
                (prefix_hbm, prefix_raw),
                (response_hbm, response_raw),
                (probe_hbm, probe),
                (offsets_hbm, offsets),
                (partner_hbm, partner),
                (labels_hbm, labels),
            )
        )
    ]
    for load in loads:
        load.start()
    load_q = pltpu.make_async_copy(queries_hbm, q_buf, local_sem.at[0])
    load_up = pltpu.make_async_copy(upstream_hbm, up_buf, local_sem.at[1])
    load_q.start()
    load_up.start()

    barrier = pltpu.get_barrier_semaphore()

    def greet(step, carry):
        pl.semaphore_signal(barrier, inc=1, device_id=place(step), device_id_type=MESH)
        return carry

    lax.fori_loop(1, n_all, greet, 0)
    loads[0].wait()
    prefix[...] = jnp.swapaxes(prefix_raw[0], 0, 1)
    pl.semaphore_wait(barrier, n_all - 1)

    def head(g):
        return slice(g * HD, (g + 1) * HD)

    def prefix_at(chunk):
        return prefix.at[chunk % 2, :, head(chunk // 2)]

    def forward_copy(chunk, kind):
        if kind == 0:
            src, dst, to = prefix_at(chunk), near[chunk].at[1 + 2 * odd], mate
        elif kind == 1:
            src, dst, to = prefix_at(chunk), near[chunk].at[4 - 4 * odd], soon
        elif kind == 2:
            src, dst, to = prefix_at(chunk), near[chunk].at[4 * odd], later
        else:
            src, dst, to = near[chunk].at[4 - 4 * odd], near[chunk].at[3 - 2 * odd], mate
        return pltpu.make_async_remote_copy(
            src_ref=src,
            dst_ref=dst,
            send_sem=fwd_send.at[chunk, kind],
            recv_sem=fwd_recv.at[chunk, kind],
            device_id={"dp": to},
            device_id_type=MESH,
        )

    fwd = [[forward_copy(c, k) for k in range(4)] for c in range(chunks)]
    for k in (1, 0, 2):
        for c in range(chunks):
            fwd[c][k].start()

    lane = lax.broadcasted_iota(jnp.int32, (1, m_len), 1)
    token = lax.rem(lane, rows)
    not_last = jnp.where(token == rows - 1, 0.0, 1.0)
    causal = lax.broadcasted_iota(jnp.int32, (rows, m_len), 0) <= lax.rem(
        lax.broadcasted_iota(jnp.int32, (rows, m_len), 1), rows
    )
    pick = jnp.where(
        lax.broadcasted_iota(jnp.int32, (LAST_ROWS, m_len), 0) * rows + (rows - 1)
        == lax.broadcasted_iota(jnp.int32, (LAST_ROWS, m_len), 1),
        1.0,
        0.0,
    ).astype(jnp.bfloat16)

    def stacked(buf, r, g):
        return jnp.concatenate(
            [buf[r, :, (g * group + h) * HD : (g * group + h + 1) * HD] for h in range(group)],
            axis=0,
        )

    def key_value(r, g, prefix_k, prefix_v):
        mine = pl.ds(pl.multiple_of(r * rows, rows), rows)
        return (
            jnp.concatenate([prefix_k, response[0, mine, head(g)]], axis=0),
            jnp.concatenate([prefix_v, response[1, mine, head(g)]], axis=0),
        )

    def probe_of(g):
        return jnp.concatenate(
            [probe[g * group : (g + 1) * group], jnp.zeros((LAST_ROWS - group, HD), jnp.float32)],
            axis=0,
        )

    def last_token(r, g, k, v):
        q31 = dot(pick, stacked(q_buf, r, g), 1, 0).astype(jnp.bfloat16)
        s = dot(q31, k, 1, 1)
        e = jnp.exp((s - jnp.max(s, axis=1, keepdims=True)) * scale)
        w = e / jnp.sum(e, axis=1, keepdims=True)
        w_low = w.astype(jnp.bfloat16)
        o = dot(w_low, v, 1, 0)
        q_last[r, g] = q31
        w_last[r, g] = w_low
        p_last[r, g] = w
        o_last[r, g] = o
        by_head = jnp.sum(o * probe_of(g), axis=1, keepdims=True)
        stats = [
            jnp.max(s, axis=1, keepdims=True),
            1.0 / jnp.sum(e, axis=1, keepdims=True),
            jnp.sum(o * dot(pick, stacked(up_buf, r, g), 1, 0), axis=1, keepdims=True),
            by_head,
        ]
        packed = jnp.zeros((LAST_ROWS, HD), jnp.float32)
        for i, stat in enumerate(stats):
            packed = packed + jnp.where(lane_of == g * len(stats) + i, stat, 0.0)
        return jnp.sum(by_head, axis=0, keepdims=True), packed

    def main(r, g, k, v):
        q = stacked(q_buf, r, g)
        d_out = stacked(up_buf, r, g)
        s = dot(k, q, 1, 1)
        s = jnp.concatenate(
            [s[:prefix_len], jnp.where(causal, s[prefix_len:], -1e30)], axis=0
        )
        e = jnp.exp((s - jnp.max(s, axis=0, keepdims=True)) * scale)
        w = e * (not_last / jnp.sum(e, axis=0, keepdims=True))
        w_low = w.astype(jnp.bfloat16)
        dw = dot(v, d_out, 1, 1)
        delta = jnp.sum(w_low.astype(jnp.float32) * dw, axis=0, keepdims=True)
        ds = (w * (dw - delta) * scale).astype(jnp.bfloat16)
        d_rows[r, 2 * g] = dot(ds, q, 1, 0)
        d_rows[r, 2 * g + 1] = dot(w_low, d_out, 1, 0)
        dq = dot(ds, k, 0, 0).astype(jnp.bfloat16)
        for h in range(group):
            gq_buf[r, :, (g * group + h) * HD : (g * group + h + 1) * HD] = dq[
                h * rows : (h + 1) * rows
            ]

    slot_row = lax.broadcasted_iota(jnp.int32, (8, HD), 0)
    lane_of = lax.broadcasted_iota(jnp.int32, (LAST_ROWS, HD), 1)

    for load in loads[1:]:
        load.wait()
    response[...] = jnp.swapaxes(
        response_raw[...].reshape(slots * rows, 2, kv_width), 0, 1
    )
    load_q.wait()
    load_up.wait()

    for g in range(heads_kv):
        for i, buf in enumerate((q_buf, up_buf)):
            both = [dot(pick, stacked(buf, r, g), 1, 0)[:group] for r in (2, 3)]
            sent_rows[i, g] = jnp.concatenate(both, axis=0).astype(jnp.bfloat16)

    def note_copy(which, to):
        src = (sent_rows, sent_stats)[which]
        dst = (got_rows, got_stats)[which].at[to]
        near_by = (1, n_dp - 1, 2, n_dp - 2)[to]
        return pltpu.make_async_remote_copy(
            src_ref=src,
            dst_ref=dst,
            send_sem=note_send.at[which, to],
            recv_sem=note_recv.at[which, to],
            device_id={"dp": lax.rem(me + near_by, n_dp)},
            device_id_type=MESH,
        )

    notes = [[note_copy(which, to) for to in range(4)] for which in range(2)]

    for c in range(chunks):
        near[c][2] = prefix[c % 2, :, head(c // 2)]
    note = jnp.zeros((8, HD), jnp.float32)
    own_stats = []
    for r in (0, 1):
        mine = jnp.zeros((LAST_ROWS, HD), jnp.float32)
        for g in range(heads_kv):
            k, v = key_value(r, g, prefix[0, :, head(g)], prefix[1, :, head(g)])
            reward, packed = last_token(r, g, k, v)
            note = note + jnp.where(slot_row == r, reward, 0.0)
            mine = mine + packed
            main(r, g, k, v)
        own_stats.append(mine[:group])
        for c in (2 * r, 2 * r + 1):
            fwd[c][1].wait_recv()
            fwd[c][3].start()
    stats_near[...] = jnp.concatenate(own_stats, axis=0)

    for to in range(4):
        notes[0][to].start()

    def backward_copy(chunk, kind):
        src = (out_a, out_b, out_c, out_d)[kind].at[chunk]
        dst = (in_a, in_b, in_c, in_d)[kind].at[chunk]
        if kind < 2:
            to = mate
        elif kind == 2:
            to = soon
        else:
            to = later
        return pltpu.make_async_remote_copy(
            src_ref=src,
            dst_ref=dst,
            send_sem=bwd_send.at[chunk, kind],
            recv_sem=bwd_recv.at[chunk, kind],
            device_id={"dp": to},
            device_id_type=MESH,
        )

    bwd = [[backward_copy(c, k) for k in range(4)] for c in range(chunks)]
    reach2 = offsets[0, 2]
    reach3 = offsets[0, 3]

    def far_keys(r, g):
        reach = offsets[0, r] + SPAN
        return key_value(r, g, near[2 * g][reach], near[2 * g + 1][reach])

    def part(d2, d3, reach):
        return jnp.where(reach2 == reach, d2, 0.0) + jnp.where(reach3 == reach, d3, 0.0)

    def pass_on(c):
        bwd[c][0].wait_recv()
        out_d[c] = (
            d_rows[3, c, :prefix_len] + in_a[c].astype(jnp.float32)
        ).astype(jnp.bfloat16)
        bwd[c][3].start()

    def reward_copy(step):
        return pltpu.make_async_remote_copy(
            src_ref=message,
            dst_ref=table.at[my_all],
            send_sem=rew_send.at[step],
            recv_sem=rew_recv.at[step],
            device_id=place(step),
            device_id_type=MESH,
        )

    def tell(step, carry):
        reward_copy(step).start()
        return carry

    far_stats = [jnp.zeros((LAST_ROWS, HD), jnp.float32)] * 2
    for g in range(heads_kv):
        for c in (2 * g, 2 * g + 1):
            fwd[c][2].wait_recv()
            fwd[c][0].wait_recv()
            fwd[c][3].wait_recv()
        for r in (2, 3):
            k, v = far_keys(r, g)
            reward, packed = last_token(r, g, k, v)
            note = note + jnp.where(slot_row == r, reward, 0.0)
            far_stats[r - 2] = far_stats[r - 2] + packed
        if g == heads_kv - 1:
            for r in (2, 3):
                note = note + jnp.where(
                    slot_row == slots + r - 2, offsets[0, r].astype(jnp.float32), 0.0
                )
            message[...] = note
            table[my_all] = note
            lax.fori_loop(1, n_all, tell, 0)
            sent_stats[...] = jnp.concatenate([x[:group] for x in far_stats], axis=0)
            for to in range(4):
                notes[1][to].start()
        for r in (2, 3):
            main(r, g, *far_keys(r, g))
        for chunk in (2 * g, 2 * g + 1):
            d2 = d_rows[2, chunk, :prefix_len]
            d3 = d_rows[3, chunk, :prefix_len]
            out_a[chunk] = part(d2, d3, 2 * odd - 1).astype(jnp.bfloat16)
            bwd[chunk][0].start()
            out_c[chunk] = part(d2, d3, 4 * odd - 2).astype(jnp.bfloat16)
            bwd[chunk][2].start()
            out_b[chunk] = part(d2, d3, 1 - 2 * odd).astype(jnp.bfloat16)
            d_rows[2, chunk, :prefix_len] = part(d2, d3, 0)
            d_rows[3, chunk, :prefix_len] = part(d2, d3, 2 - 4 * odd)
    for c in range(chunks):
        pass_on(c)
    for c in range(chunks):
        bwd[c][0].wait_send()
        bwd[c][1].start()

    def hear(step, carry):
        reward_copy(step).wait()
        return carry

    lax.fori_loop(1, n_all, hear, 0)

    summed = jnp.sum(table[...].reshape(n_dp, n_tensor, 8, HD), axis=1).reshape(n_dp * 8, HD)
    reward_sum[...] = summed
    resp = partner.shape[1]
    other = partner[...]
    label = labels[...]
    all_rows = lax.broadcasted_iota(jnp.int32, (n_dp * 8, resp), 0)
    all_ids = lax.rem(all_rows, 8) + lax.div(all_rows, 8) * slots
    all_ids = jnp.where(lax.rem(all_rows, 8) < slots, all_ids, -1)
    pair = lax.broadcasted_iota(jnp.int32, (n_dp * 8, resp), 1)
    column = summed[:, :1]
    first = jnp.sum(jnp.where(all_ids == pair, column, 0.0), axis=0, keepdims=True)
    second = jnp.sum(jnp.where(all_ids == other, column, 0.0), axis=0, keepdims=True)
    middle = 0.5 * (first + second)
    exp_first = jnp.exp(first)
    exp_second = jnp.exp(second)
    exp_middle = jnp.exp(middle)
    totals = exp_first + exp_second + exp_middle
    chosen = jnp.where(label == 0, first, jnp.where(label == 1, second, middle))
    loss = jnp.sum(jnp.log(totals) - chosen, axis=1, keepdims=True) * (1.0 / resp)
    loss_out[0] = loss[0, 0]
    tie_share = 0.5 * exp_middle / totals
    half_tie = jnp.where(label == 2, 0.5, 0.0)
    grad_first = exp_first / totals + tie_share - jnp.where(label == 0, 1.0, 0.0) - half_tie
    grad_second = exp_second / totals + tie_share - jnp.where(label == 1, 1.0, 0.0) - half_tie

    def gradient_of(ids):
        at = lax.broadcasted_iota(jnp.int32, (ids.shape[0], resp), 1)
        return jnp.sum(
            jnp.where(ids == at, grad_first, 0.0) + jnp.where(ids == other, grad_second, 0.0),
            axis=1,
            keepdims=True,
        )

    own = reward_sum[pl.ds(pl.multiple_of(me * 8, 8), 8)]
    for j in range(slots):
        rewards_out[j] = own[j, 0]

    def finish(r, g, k, v):
        mine = gradient_of(jnp.full((LAST_ROWS, resp), me * slots + r, jnp.int32))
        up31 = dot(pick, stacked(up_buf, r, g), 1, 0)
        d31 = (up31 + mine * probe_of(g)).astype(jnp.bfloat16)
        dw = dot(d31, v, 1, 1)
        delta = jnp.sum(d31.astype(jnp.float32) * o_last[r, g], axis=1, keepdims=True)
        ds = (p_last[r, g] * (dw - delta) * scale).astype(jnp.bfloat16)
        dk = d_rows[r, 2 * g, prefix_len:] + dot(ds[:, prefix_len:], q_last[r, g], 0, 0)
        dv = d_rows[r, 2 * g + 1, prefix_len:] + dot(w_last[r, g][:, prefix_len:], d31, 0, 0)
        dq = dot(pick, dot(ds, k, 1, 0).astype(jnp.bfloat16), 0, 0).astype(jnp.bfloat16)
        for h in range(group):
            cols = slice((g * group + h) * HD, (g * group + h + 1) * HD)
            gq_buf[r, :, cols] = gq_buf[r, :, cols] + dq[h * rows : (h + 1) * rows]
        mine_rows = slice(r * rows, (r + 1) * rows)
        grad_r[0, mine_rows, head(g)] = dk.astype(jnp.bfloat16)
        grad_r[1, mine_rows, head(g)] = dv.astype(jnp.bfloat16)

    for g in range(heads_kv):
        for r in range(slots):
            if r < 2:
                finish(r, g, *key_value(r, g, prefix[0, :, head(g)], prefix[1, :, head(g)]))
            else:
                finish(r, g, *far_keys(r, g))
    grad_r_out[...] = jnp.swapaxes(grad_r[...], 0, 1).reshape(grad_r_out.shape)
    store_q = pltpu.make_async_copy(gq_buf, grad_q_hbm, local_sem.at[2])
    store_q.start()

    near_by = (0, 0, -1, 1, -2, 2)
    pair_rows = lax.broadcasted_iota(jnp.int32, (2 * group, resp), 0)
    second_slot = pair_rows >= group
    grad_rows = []
    used = []
    for i, reach in enumerate(near_by):
        device = lax.rem(me + n_dp + reach, n_dp)
        first_slot = 0 if i == 0 else 2
        ids = jnp.where(second_slot, 1, 0) + (device * slots + first_slot)
        grad_rows.append(gradient_of(ids))
        if i == 0:
            used.append(jnp.ones((2 * group, 1), jnp.float32))
        else:
            told = table[device * n_tensor]
            offset = jnp.where(
                second_slot[:, :1], told[slots + 1 : slots + 2, :1], told[slots : slots + 1, :1]
            )
            used.append(jnp.where(offset == float(-reach), 1.0, 0.0))
    grad_rows = jnp.concatenate(grad_rows, axis=0)
    used = jnp.concatenate(used, axis=0)
    for which in range(2):
        for to in range(4):
            notes[which][to].wait_recv()
    stats = jnp.concatenate(
        [stats_near[...], sent_stats[...]] + [got_stats[to] for to in range(4)], axis=0
    )
    for g in range(heads_kv):
        q31 = jnp.concatenate(
            [jnp.concatenate([q_last[0, g][:group], q_last[1, g][:group]], axis=0), sent_rows[0, g]]
            + [got_rows[to, 0, g] for to in range(4)],
            axis=0,
        )
        near_up = [dot(pick, stacked(up_buf, r, g), 1, 0)[:group] for r in (0, 1)]
        up31 = jnp.concatenate(
            near_up
            + [sent_rows[1, g].astype(jnp.float32)]
            + [got_rows[to, 1, g].astype(jnp.float32) for to in range(4)],
            axis=0,
        )
        probes = jnp.concatenate([probe[g * group : (g + 1) * group]] * (2 * len(near_by)), axis=0)
        top, inverse, up_o, probe_o = [stats[:, 4 * g + i : 4 * g + i + 1] for i in range(4)]
        k, v = prefix[0, :, head(g)], prefix[1, :, head(g)]
        d31 = (up31 + grad_rows * probes).astype(jnp.bfloat16)
        w = jnp.where(used > 0.0, jnp.exp((dot(q31, k, 1, 1) - top) * scale) * inverse, 0.0)
        dw = dot(d31, v, 1, 1)
        ds = (w * (dw - (up_o + grad_rows * probe_o)) * scale).astype(jnp.bfloat16)
        d_rows[2, 2 * g, :prefix_len] += (
            d_rows[0, 2 * g, :prefix_len] + d_rows[1, 2 * g, :prefix_len] + dot(ds, q31, 0, 0)
        )
        d_rows[2, 2 * g + 1, :prefix_len] += (
            d_rows[0, 2 * g + 1, :prefix_len]
            + d_rows[1, 2 * g + 1, :prefix_len]
            + dot(w.astype(jnp.bfloat16), d31, 0, 0)
        )

    for c in range(chunks):
        for k in range(4):
            fwd[c][k].wait_send()
    for c in range(chunks):
        bwd[c][1].wait_recv()
        bwd[c][2].wait_recv()
        bwd[c][3].wait_recv()
        prefix[c % 2, :, head(c // 2)] = (
            d_rows[2, c, :prefix_len]
            + in_b[c].astype(jnp.float32)
            + in_c[c].astype(jnp.float32)
            + in_d[c].astype(jnp.float32)
        ).astype(jnp.bfloat16)

    for c in range(chunks):
        for k in (1, 2, 3):
            bwd[c][k].wait_send()
    grad_p_out[...] = jnp.swapaxes(prefix[...], 0, 1)[None]
    for which in range(2):
        for to in range(4):
            notes[which][to].wait_send()
    store_q.wait()


def hand_over(*refs):
    count = len(refs) // 2
    for i in range(count):
        if refs[i].ndim > 1:
            refs[count + i][...] = refs[i][...]
        else:
            for j in range(refs[i].shape[0]):
                refs[count + i][j] = refs[i][j]


def per_device(
    n_dp,
    n_tensor,
    queries,
    response_cache,
    prefix_cache,
    upstream,
    reward_probe,
    slot_offsets,
    partner,
    labels,
):
    slots, rows, width = queries.shape
    prefix_len = prefix_cache.shape[1]
    kv_heads = response_cache.shape[3] // HD
    chunks = 2 * kv_heads
    keys = prefix_len + rows
    group = width // HD // kv_heads
    resp = partner.shape[0]
    n_all = n_dp * n_tensor
    kv_width = kv_heads * HD
    kv_width = kv_heads * HD
    vmem = pl.BlockSpec(memory_space=pltpu.VMEM)
    smem = pl.BlockSpec(memory_space=pltpu.SMEM)
    hbm = pl.BlockSpec(memory_space=pl.ANY)
    near = pltpu.VMEM((2 * SPAN + 1, prefix_len, HD), jnp.bfloat16)
    block = pltpu.VMEM((chunks, prefix_len, HD), jnp.bfloat16)
    rewards, loss, grad_q, grad_r, grad_p = pl.pallas_call(
        functools.partial(kernel, n_dp, n_tensor),
        out_shape=(
            jax.ShapeDtypeStruct((slots,), jnp.float32),
            jax.ShapeDtypeStruct((1,), jnp.float32),
            jax.ShapeDtypeStruct(queries.shape, jnp.bfloat16),
            jax.ShapeDtypeStruct(response_cache.shape, jnp.bfloat16),
            jax.ShapeDtypeStruct(prefix_cache.shape, jnp.bfloat16),
        ),
        in_specs=[hbm] * 8,
        out_specs=(smem, smem, hbm, vmem, vmem),
        scratch_shapes=[
            pltpu.VMEM(prefix_cache.shape, jnp.bfloat16),
            pltpu.VMEM(response_cache.shape, jnp.bfloat16),
            pltpu.VMEM((width // HD, HD), jnp.float32),
            pltpu.VMEM((1, resp), jnp.int32),
            pltpu.VMEM((1, resp), jnp.int32),
            pltpu.SMEM((1, slots), jnp.int32),
            pltpu.VMEM((2, prefix_len, kv_width), jnp.bfloat16),
            pltpu.VMEM((2, slots * rows, kv_width), jnp.bfloat16),
            pltpu.VMEM((2, slots * rows, kv_width), jnp.bfloat16),
            pltpu.VMEM(queries.shape, jnp.bfloat16),
            pltpu.VMEM(queries.shape, jnp.bfloat16),
            pltpu.VMEM(queries.shape, jnp.bfloat16),
            near,
            near,
            near,
            near,
            pltpu.VMEM((slots, chunks, keys, HD), jnp.float32),
            pltpu.VMEM((slots, kv_heads, LAST_ROWS, keys), jnp.bfloat16),
            pltpu.VMEM((slots, kv_heads, LAST_ROWS, keys), jnp.float32),
            pltpu.VMEM((slots, kv_heads, LAST_ROWS, HD), jnp.float32),
            pltpu.VMEM((slots, kv_heads, LAST_ROWS, HD), jnp.bfloat16),
            pltpu.VMEM((8, HD), jnp.float32),
            pltpu.VMEM((n_all, 8, HD), jnp.float32),
            pltpu.VMEM((n_dp * 8, HD), jnp.float32),
            pltpu.VMEM((2, kv_heads, 2 * group, HD), jnp.bfloat16),
            pltpu.VMEM((4, 2, kv_heads, 2 * group, HD), jnp.bfloat16),
            pltpu.VMEM((2 * group, HD), jnp.float32),
            pltpu.VMEM((4, 2 * group, HD), jnp.float32),
            pltpu.VMEM((2 * group, HD), jnp.float32),
            block,
            block,
            block,
            block,
            block,
            block,
            block,
            block,
            pltpu.SemaphoreType.DMA((9,)),
            pltpu.SemaphoreType.DMA((chunks, 4)),
            pltpu.SemaphoreType.DMA((chunks, 4)),
            pltpu.SemaphoreType.DMA((chunks, 4)),
            pltpu.SemaphoreType.DMA((chunks, 4)),
            pltpu.SemaphoreType.DMA((n_all,)),
            pltpu.SemaphoreType.DMA((n_all,)),
            pltpu.SemaphoreType.DMA((2, 4)),
            pltpu.SemaphoreType.DMA((2, 4)),
        ],
        compiler_params=pltpu.CompilerParams(
            collective_id=0, has_side_effects=True, vmem_limit_bytes=60 * 1024 * 1024
        ),
    )(
        slot_offsets,
        queries,
        upstream,
        prefix_cache,
        response_cache,
        reward_probe.reshape(width // HD, HD),
        partner.reshape(1, resp),
        labels.reshape(1, resp),
    )
    results = [rewards, loss, grad_q, grad_r, grad_p]
    moved = (0, 1, 2, 3, 4)
    taken = [results[i] for i in moved]
    given = pl.pallas_call(
        hand_over,
        out_shape=tuple(jax.ShapeDtypeStruct(x.shape, x.dtype) for x in taken),
        in_specs=[smem if x.ndim == 1 else vmem for x in taken],
        out_specs=tuple(smem if x.ndim == 1 else vmem for x in taken),
    )(*taken)
    for i, value in zip(moved, given):
        results[i] = value
    return tuple(results)


def solution(mesh):
    in_specs = (
        P(("group", "dp"), None, "tensor"),
        P(("group", "dp"), None, None, "tensor"),
        P(("group", "dp"), None, None, "tensor"),
        P(("group", "dp"), None, "tensor"),
        P("tensor"),
        P(("group", "dp"), None),
        P("group"),
        P("group"),
    )
    out_specs = (
        P(("group", "dp")),
        P("group"),
        P(("group", "dp"), None, "tensor"),
        P(("group", "dp"), None, None, "tensor"),
        P(("group", "dp"), None, None, "tensor"),
    )
    return jax.shard_map(
        functools.partial(per_device, mesh.shape["dp"], mesh.shape["tensor"]),
        mesh=mesh,
        in_specs=in_specs,
        out_specs=out_specs,
        check_vma=False,
    )
```

```python
import functools
import math

import jax
import jax.numpy as jnp
from jax import lax
from jax.experimental import pallas as pl
from jax.experimental.pallas import tpu as pltpu
from jax.sharding import PartitionSpec as P

HD = 128
SPAN = 2
LAST_ROWS = 16
MESH = pl.DeviceIdType.MESH


def dot(a, b, contract_a, contract_b):
    return lax.dot_general(
        a, b, (((contract_a,), (contract_b,)), ((), ())), preferred_element_type=jnp.float32
    )


def kernel(
    n_dp,
    n_tensor,
    offsets_hbm,
    queries_hbm,
    upstream_hbm,
    prefix_hbm,
    response_hbm,
    probe_hbm,
    partner_hbm,
    labels_hbm,
    rewards_out,
    loss_out,
    grad_q_hbm,
    grad_r_out,
    grad_p_out,
    prefix_raw,
    response_raw,
    probe,
    partner,
    labels,
    offsets,
    prefix,
    response,
    grad_r,
    q_buf,
    up_buf,
    gq_buf,
    near0,
    near1,
    near2,
    near3,
    d_rows,
    w_last,
    p_last,
    o_last,
    q_last,
    u_last,
    message,
    table,
    reward_sum,
    sent_rows,
    got_rows,
    sent_stats,
    got_stats,
    stats_near,
    out_a,
    out_b,
    out_c,
    out_d,
    in_a,
    in_b,
    in_c,
    in_d,
    local_sem,
    fwd_send,
    fwd_recv,
    bwd_send,
    bwd_recv,
    rew_send,
    rew_recv,
    note_send,
    note_recv,
):
    slots, rows, width = q_buf.shape
    _, prefix_len, kv_width = prefix.shape
    heads_kv = kv_width // HD
    chunks = 2 * heads_kv
    group = width // HD // heads_kv
    keys = prefix_len + rows
    m_len = group * rows
    near = (near0, near1, near2, near3)
    scale = 1.0 / math.sqrt(HD)

    me = lax.axis_index("dp")
    my_t = lax.axis_index("tensor")
    odd = lax.rem(me, 2)
    mate = me + 1 - 2 * odd
    soon = lax.rem(me + n_dp - 2 + 4 * odd, n_dp)
    later = lax.rem(me + n_dp + 2 - 4 * odd, n_dp)
    n_all = n_dp * n_tensor
    my_all = me * n_tensor + my_t

    def place(step):
        other = lax.rem(my_all + step, n_all)
        return {"dp": lax.div(other, n_tensor), "tensor": lax.rem(other, n_tensor)}

    loads = [
        pltpu.make_async_copy(src, dst, local_sem.at[3 + i])
        for i, (src, dst) in enumerate(
            (
                (prefix_hbm, prefix_raw),
                (response_hbm, response_raw),
                (probe_hbm, probe),
                (offsets_hbm, offsets),
                (partner_hbm, partner),
                (labels_hbm, labels),
            )
        )
    ]
    for load in loads:
        load.start()
    load_q = pltpu.make_async_copy(queries_hbm, q_buf, local_sem.at[0])
    load_up = pltpu.make_async_copy(upstream_hbm, up_buf, local_sem.at[1])
    load_q.start()
    load_up.start()

    barrier = pltpu.get_barrier_semaphore()

    def greet(step, carry):
        pl.semaphore_signal(barrier, inc=1, device_id=place(step), device_id_type=MESH)
        return carry

    lax.fori_loop(1, n_all, greet, 0)
    loads[0].wait()
    prefix[...] = jnp.swapaxes(prefix_raw[0], 0, 1)
    pl.semaphore_wait(barrier, n_all - 1)

    def head(g):
        return slice(g * HD, (g + 1) * HD)

    def prefix_at(chunk):
        return prefix.at[chunk % 2, :, head(chunk // 2)]

    def forward_copy(chunk, kind):
        if kind == 0:
            src, dst, to = prefix_at(chunk), near[chunk].at[1 + 2 * odd], mate
        elif kind == 1:
            src, dst, to = prefix_at(chunk), near[chunk].at[4 - 4 * odd], soon
        elif kind == 2:
            src, dst, to = prefix_at(chunk), near[chunk].at[4 * odd], later
        else:
            src, dst, to = near[chunk].at[4 - 4 * odd], near[chunk].at[3 - 2 * odd], mate
        return pltpu.make_async_remote_copy(
            src_ref=src,
            dst_ref=dst,
            send_sem=fwd_send.at[chunk, kind],
            recv_sem=fwd_recv.at[chunk, kind],
            device_id={"dp": to},
            device_id_type=MESH,
        )

    fwd = [[forward_copy(c, k) for k in range(4)] for c in range(chunks)]
    for k in (1, 0, 2):
        for c in range(chunks):
            fwd[c][k].start()

    lane = lax.broadcasted_iota(jnp.int32, (1, m_len), 1)
    token = lax.rem(lane, rows)
    not_last = jnp.where(token == rows - 1, 0.0, 1.0)
    causal = lax.broadcasted_iota(jnp.int32, (rows, m_len), 0) <= lax.rem(
        lax.broadcasted_iota(jnp.int32, (rows, m_len), 1), rows
    )
    pick = jnp.where(
        lax.broadcasted_iota(jnp.int32, (LAST_ROWS, m_len), 0) * rows + (rows - 1)
        == lax.broadcasted_iota(jnp.int32, (LAST_ROWS, m_len), 1),
        1.0,
        0.0,
    ).astype(jnp.bfloat16)

    def stacked(buf, r, g):
        return jnp.concatenate(
            [buf[r, :, (g * group + h) * HD : (g * group + h + 1) * HD] for h in range(group)],
            axis=0,
        )

    def key_value(r, g, prefix_k, prefix_v):
        mine = pl.ds(pl.multiple_of(r * rows, rows), rows)
        return (
            jnp.concatenate([prefix_k, response[0, mine, head(g)]], axis=0),
            jnp.concatenate([prefix_v, response[1, mine, head(g)]], axis=0),
        )

    def probe_of(g):
        return jnp.concatenate(
            [probe[g * group : (g + 1) * group], jnp.zeros((LAST_ROWS - group, HD), jnp.float32)],
            axis=0,
        )

    def last_token(r, g, k, v):
        q31 = dot(pick, stacked(q_buf, r, g), 1, 0).astype(jnp.bfloat16)
        s = dot(q31, k, 1, 1)
        e = jnp.exp((s - jnp.max(s, axis=1, keepdims=True)) * scale)
        w = e / jnp.sum(e, axis=1, keepdims=True)
        w_low = w.astype(jnp.bfloat16)
        o = dot(w_low, v, 1, 0)
        q_last[r, g] = q31
        w_last[r, g] = w_low
        p_last[r, g] = w
        o_last[r, g] = o
        up31 = dot(pick, stacked(up_buf, r, g), 1, 0)
        u_last[r, g] = up31
        by_head = jnp.sum(o * probe_of(g), axis=1, keepdims=True)
        stats = [
            jnp.max(s, axis=1, keepdims=True),
            1.0 / jnp.sum(e, axis=1, keepdims=True),
            jnp.sum(o * up31, axis=1, keepdims=True),
            by_head,
        ]
        packed = jnp.zeros((LAST_ROWS, HD), jnp.float32)
        for i, stat in enumerate(stats):
            packed = packed + jnp.where(lane_of == g * len(stats) + i, stat, 0.0)
        return jnp.sum(by_head, axis=0, keepdims=True), packed

    def main(r, g, k, v):
        q = stacked(q_buf, r, g)
        d_out = stacked(up_buf, r, g)
        s = dot(k, q, 1, 1)
        s = jnp.concatenate(
            [s[:prefix_len], jnp.where(causal, s[prefix_len:], -1e30)], axis=0
        )
        e = jnp.exp((s - jnp.max(s, axis=0, keepdims=True)) * scale)
        w = e * (not_last / jnp.sum(e, axis=0, keepdims=True))
        w_low = w.astype(jnp.bfloat16)
        dw = dot(v, d_out, 1, 1)
        delta = jnp.sum(w_low.astype(jnp.float32) * dw, axis=0, keepdims=True)
        ds = (w * (dw - delta) * scale).astype(jnp.bfloat16)
        d_rows[r, 2 * g] = dot(ds, q, 1, 0)
        d_rows[r, 2 * g + 1] = dot(w_low, d_out, 1, 0)
        dq = dot(ds, k, 0, 0).astype(jnp.bfloat16)
        for h in range(group):
            gq_buf[r, :, (g * group + h) * HD : (g * group + h + 1) * HD] = dq[
                h * rows : (h + 1) * rows
            ]

    slot_row = lax.broadcasted_iota(jnp.int32, (8, HD), 0)
    lane_of = lax.broadcasted_iota(jnp.int32, (LAST_ROWS, HD), 1)

    for load in loads[1:]:
        load.wait()
    response[...] = jnp.swapaxes(
        response_raw[...].reshape(slots * rows, 2, kv_width), 0, 1
    )
    load_q.wait()
    load_up.wait()

    for g in range(heads_kv):
        for i, buf in enumerate((q_buf, up_buf)):
            both = [dot(pick, stacked(buf, r, g), 1, 0)[:group] for r in (2, 3)]
            sent_rows[i, g] = jnp.concatenate(both, axis=0).astype(jnp.bfloat16)

    def note_copy(which, to):
        src = (sent_rows, sent_stats)[which]
        dst = (got_rows, got_stats)[which].at[to]
        near_by = (1, n_dp - 1, 2, n_dp - 2)[to]
        return pltpu.make_async_remote_copy(
            src_ref=src,
            dst_ref=dst,
            send_sem=note_send.at[which, to],
            recv_sem=note_recv.at[which, to],
            device_id={"dp": lax.rem(me + near_by, n_dp)},
            device_id_type=MESH,
        )

    notes = [[note_copy(which, to) for to in range(4)] for which in range(2)]

    for c in range(chunks):
        near[c][2] = prefix[c % 2, :, head(c // 2)]
    note = jnp.zeros((8, HD), jnp.float32)
    own_stats = []
    for r in (0, 1):
        mine = jnp.zeros((LAST_ROWS, HD), jnp.float32)
        for g in range(heads_kv):
            k, v = key_value(r, g, prefix[0, :, head(g)], prefix[1, :, head(g)])
            reward, packed = last_token(r, g, k, v)
            note = note + jnp.where(slot_row == r, reward, 0.0)
            mine = mine + packed
            main(r, g, k, v)
        own_stats.append(mine[:group])
        for c in (2 * r, 2 * r + 1):
            fwd[c][1].wait_recv()
            fwd[c][3].start()
    stats_near[...] = jnp.concatenate(own_stats, axis=0)

    for to in range(4):
        notes[0][to].start()

    def backward_copy(chunk, kind):
        src = (out_a, out_b, out_c, out_d)[kind].at[chunk]
        dst = (in_a, in_b, in_c, in_d)[kind].at[chunk]
        if kind < 2:
            to = mate
        elif kind == 2:
            to = soon
        else:
            to = later
        return pltpu.make_async_remote_copy(
            src_ref=src,
            dst_ref=dst,
            send_sem=bwd_send.at[chunk, kind],
            recv_sem=bwd_recv.at[chunk, kind],
            device_id={"dp": to},
            device_id_type=MESH,
        )

    bwd = [[backward_copy(c, k) for k in range(4)] for c in range(chunks)]
    reach2 = offsets[0, 2]
    reach3 = offsets[0, 3]

    def far_keys(r, g):
        reach = offsets[0, r] + SPAN
        return key_value(r, g, near[2 * g][reach], near[2 * g + 1][reach])

    def part(d2, d3, reach):
        return jnp.where(reach2 == reach, d2, 0.0) + jnp.where(reach3 == reach, d3, 0.0)

    def pass_on(c):
        bwd[c][0].wait_recv()
        out_d[c] = (
            d_rows[3, c, :prefix_len] + in_a[c].astype(jnp.float32)
        ).astype(jnp.bfloat16)
        bwd[c][3].start()

    def reward_copy(step):
        return pltpu.make_async_remote_copy(
            src_ref=message,
            dst_ref=table.at[my_all],
            send_sem=rew_send.at[step],
            recv_sem=rew_recv.at[step],
            device_id=place(step),
            device_id_type=MESH,
        )

    def tell(step, carry):
        reward_copy(step).start()
        return carry

    far_stats = [jnp.zeros((LAST_ROWS, HD), jnp.float32)] * 2
    for g in range(heads_kv):
        for c in (2 * g, 2 * g + 1):
            fwd[c][2].wait_recv()
            fwd[c][0].wait_recv()
            fwd[c][3].wait_recv()
        for r in (2, 3):
            k, v = far_keys(r, g)
            reward, packed = last_token(r, g, k, v)
            note = note + jnp.where(slot_row == r, reward, 0.0)
            far_stats[r - 2] = far_stats[r - 2] + packed
        if g == heads_kv - 1:
            for r in (2, 3):
                note = note + jnp.where(
                    slot_row == slots + r - 2, offsets[0, r].astype(jnp.float32), 0.0
                )
            message[...] = note
            table[my_all] = note
            lax.fori_loop(1, n_all, tell, 0)
            sent_stats[...] = jnp.concatenate([x[:group] for x in far_stats], axis=0)
            for to in range(4):
                notes[1][to].start()
        for r in (2, 3):
            main(r, g, *far_keys(r, g))
        for chunk in (2 * g, 2 * g + 1):
            d2 = d_rows[2, chunk, :prefix_len]
            d3 = d_rows[3, chunk, :prefix_len]
            out_a[chunk] = part(d2, d3, 2 * odd - 1).astype(jnp.bfloat16)
            bwd[chunk][0].start()
            out_c[chunk] = part(d2, d3, 4 * odd - 2).astype(jnp.bfloat16)
            bwd[chunk][2].start()
            out_b[chunk] = part(d2, d3, 1 - 2 * odd).astype(jnp.bfloat16)
            d_rows[2, chunk, :prefix_len] = part(d2, d3, 0)
            d_rows[3, chunk, :prefix_len] = part(d2, d3, 2 - 4 * odd)
    for c in range(chunks):
        pass_on(c)
    for c in range(chunks):
        bwd[c][0].wait_send()
        bwd[c][1].start()

    def hear(step, carry):
        reward_copy(step).wait()
        return carry

    lax.fori_loop(1, n_all, hear, 0)

    summed = jnp.sum(table[...].reshape(n_dp, n_tensor, 8, HD), axis=1).reshape(n_dp * 8, HD)
    reward_sum[...] = summed
    resp = partner.shape[1]
    other = partner[...]
    label = labels[...]
    all_rows = lax.broadcasted_iota(jnp.int32, (n_dp * 8, resp), 0)
    all_ids = lax.rem(all_rows, 8) + lax.div(all_rows, 8) * slots
    all_ids = jnp.where(lax.rem(all_rows, 8) < slots, all_ids, -1)
    pair = lax.broadcasted_iota(jnp.int32, (n_dp * 8, resp), 1)
    column = summed[:, :1]
    first = jnp.sum(jnp.where(all_ids == pair, column, 0.0), axis=0, keepdims=True)
    second = jnp.sum(jnp.where(all_ids == other, column, 0.0), axis=0, keepdims=True)
    middle = 0.5 * (first + second)
    exp_first = jnp.exp(first)
    exp_second = jnp.exp(second)
    exp_middle = jnp.exp(middle)
    totals = exp_first + exp_second + exp_middle
    chosen = jnp.where(label == 0, first, jnp.where(label == 1, second, middle))
    loss = jnp.sum(jnp.log(totals) - chosen, axis=1, keepdims=True) * (1.0 / resp)
    loss_out[0] = loss[0, 0]
    tie_share = 0.5 * exp_middle / totals
    half_tie = jnp.where(label == 2, 0.5, 0.0)
    grad_first = exp_first / totals + tie_share - jnp.where(label == 0, 1.0, 0.0) - half_tie
    grad_second = exp_second / totals + tie_share - jnp.where(label == 1, 1.0, 0.0) - half_tie

    def gradient_of(ids):
        at = lax.broadcasted_iota(jnp.int32, (ids.shape[0], resp), 1)
        return jnp.sum(
            jnp.where(ids == at, grad_first, 0.0) + jnp.where(ids == other, grad_second, 0.0),
            axis=1,
            keepdims=True,
        )

    own = reward_sum[pl.ds(pl.multiple_of(me * 8, 8), 8)]
    for j in range(slots):
        rewards_out[j] = own[j, 0]

    last_of_tile = lax.broadcasted_iota(jnp.int32, (16, HD), 0) == 15

    def finish(r, g, k, v):
        mine = gradient_of(jnp.full((LAST_ROWS, resp), me * slots + r, jnp.int32))
        d31 = (u_last[r, g] + mine * probe_of(g)).astype(jnp.bfloat16)
        dw = dot(d31, v, 1, 1)
        delta = jnp.sum(d31.astype(jnp.float32) * o_last[r, g], axis=1, keepdims=True)
        ds = (p_last[r, g] * (dw - delta) * scale).astype(jnp.bfloat16)
        dk = d_rows[r, 2 * g, prefix_len:] + dot(ds[:, prefix_len:], q_last[r, g], 0, 0)
        dv = d_rows[r, 2 * g + 1, prefix_len:] + dot(w_last[r, g][:, prefix_len:], d31, 0, 0)
        dq = dot(ds, k, 1, 0)
        for h in range(group):
            cols = slice((g * group + h) * HD, (g * group + h + 1) * HD)
            old = gq_buf[r, rows - 16 :, cols].astype(jnp.float32)
            gq_buf[r, rows - 16 :, cols] = jnp.where(
                last_of_tile, dq[h : h + 1], old
            ).astype(jnp.bfloat16)
        mine_rows = slice(r * rows, (r + 1) * rows)
        grad_r[0, mine_rows, head(g)] = dk.astype(jnp.bfloat16)
        grad_r[1, mine_rows, head(g)] = dv.astype(jnp.bfloat16)

    for g in range(heads_kv):
        for r in range(slots):
            if r < 2:
                finish(r, g, *key_value(r, g, prefix[0, :, head(g)], prefix[1, :, head(g)]))
            else:
                finish(r, g, *far_keys(r, g))
    grad_r_out[...] = jnp.swapaxes(grad_r[...], 0, 1).reshape(grad_r_out.shape)
    store_q = pltpu.make_async_copy(gq_buf, grad_q_hbm, local_sem.at[2])
    store_q.start()

    near_by = (0, 0, -1, 1, -2, 2)
    pair_rows = lax.broadcasted_iota(jnp.int32, (2 * group, resp), 0)
    second_slot = pair_rows >= group
    grad_rows = []
    used = []
    for i, reach in enumerate(near_by):
        device = lax.rem(me + n_dp + reach, n_dp)
        first_slot = 0 if i == 0 else 2
        ids = jnp.where(second_slot, 1, 0) + (device * slots + first_slot)
        grad_rows.append(gradient_of(ids))
        if i == 0:
            used.append(jnp.ones((2 * group, 1), jnp.float32))
        else:
            told = table[device * n_tensor]
            offset = jnp.where(
                second_slot[:, :1], told[slots + 1 : slots + 2, :1], told[slots : slots + 1, :1]
            )
            used.append(jnp.where(offset == float(-reach), 1.0, 0.0))
    grad_rows = jnp.concatenate(grad_rows, axis=0)
    used = jnp.concatenate(used, axis=0)
    for which in range(2):
        for to in range(4):
            notes[which][to].wait_recv()
    stats = jnp.concatenate(
        [stats_near[...], sent_stats[...]] + [got_stats[to] for to in range(4)], axis=0
    )
    for g in range(heads_kv):
        q31 = jnp.concatenate(
            [jnp.concatenate([q_last[0, g][:group], q_last[1, g][:group]], axis=0), sent_rows[0, g]]
            + [got_rows[to, 0, g] for to in range(4)],
            axis=0,
        )
        near_up = [u_last[r, g][:group] for r in (0, 1)]
        up31 = jnp.concatenate(
            near_up
            + [sent_rows[1, g].astype(jnp.float32)]
            + [got_rows[to, 1, g].astype(jnp.float32) for to in range(4)],
            axis=0,
        )
        probes = jnp.concatenate([probe[g * group : (g + 1) * group]] * (2 * len(near_by)), axis=0)
        top, inverse, up_o, probe_o = [stats[:, 4 * g + i : 4 * g + i + 1] for i in range(4)]
        k, v = prefix[0, :, head(g)], prefix[1, :, head(g)]
        d31 = (up31 + grad_rows * probes).astype(jnp.bfloat16)
        w = jnp.where(used > 0.0, jnp.exp((dot(q31, k, 1, 1) - top) * scale) * inverse, 0.0)
        dw = dot(d31, v, 1, 1)
        ds = (w * (dw - (up_o + grad_rows * probe_o)) * scale).astype(jnp.bfloat16)
        d_rows[2, 2 * g, :prefix_len] += (
            d_rows[0, 2 * g, :prefix_len] + d_rows[1, 2 * g, :prefix_len] + dot(ds, q31, 0, 0)
        )
        d_rows[2, 2 * g + 1, :prefix_len] += (
            d_rows[0, 2 * g + 1, :prefix_len]
            + d_rows[1, 2 * g + 1, :prefix_len]
            + dot(w.astype(jnp.bfloat16), d31, 0, 0)
        )

    for c in range(chunks):
        for k in range(4):
            fwd[c][k].wait_send()
    for c in range(chunks):
        bwd[c][1].wait_recv()
        bwd[c][2].wait_recv()
        bwd[c][3].wait_recv()
        prefix[c % 2, :, head(c // 2)] = (
            d_rows[2, c, :prefix_len]
            + in_b[c].astype(jnp.float32)
            + in_c[c].astype(jnp.float32)
            + in_d[c].astype(jnp.float32)
        ).astype(jnp.bfloat16)

    for c in range(chunks):
        for k in (1, 2, 3):
            bwd[c][k].wait_send()
    grad_p_out[...] = jnp.swapaxes(prefix[...], 0, 1)[None]
    for which in range(2):
        for to in range(4):
            notes[which][to].wait_send()
    store_q.wait()


def hand_over(*refs):
    count = len(refs) // 2
    for i in range(count):
        if refs[i].ndim > 1:
            refs[count + i][...] = refs[i][...]
        else:
            for j in range(refs[i].shape[0]):
                refs[count + i][j] = refs[i][j]


def per_device(
    n_dp,
    n_tensor,
    queries,
    response_cache,
    prefix_cache,
    upstream,
    reward_probe,
    slot_offsets,
    partner,
    labels,
):
    slots, rows, width = queries.shape
    prefix_len = prefix_cache.shape[1]
    kv_heads = response_cache.shape[3] // HD
    chunks = 2 * kv_heads
    keys = prefix_len + rows
    group = width // HD // kv_heads
    resp = partner.shape[0]
    n_all = n_dp * n_tensor
    kv_width = kv_heads * HD
    kv_width = kv_heads * HD
    vmem = pl.BlockSpec(memory_space=pltpu.VMEM)
    smem = pl.BlockSpec(memory_space=pltpu.SMEM)
    hbm = pl.BlockSpec(memory_space=pl.ANY)
    near = pltpu.VMEM((2 * SPAN + 1, prefix_len, HD), jnp.bfloat16)
    block = pltpu.VMEM((chunks, prefix_len, HD), jnp.bfloat16)
    rewards, loss, grad_q, grad_r, grad_p = pl.pallas_call(
        functools.partial(kernel, n_dp, n_tensor),
        out_shape=(
            jax.ShapeDtypeStruct((slots,), jnp.float32),
            jax.ShapeDtypeStruct((1,), jnp.float32),
            jax.ShapeDtypeStruct(queries.shape, jnp.bfloat16),
            jax.ShapeDtypeStruct(response_cache.shape, jnp.bfloat16),
            jax.ShapeDtypeStruct(prefix_cache.shape, jnp.bfloat16),
        ),
        in_specs=[hbm] * 8,
        out_specs=(smem, smem, hbm, vmem, vmem),
        scratch_shapes=[
            pltpu.VMEM(prefix_cache.shape, jnp.bfloat16),
            pltpu.VMEM(response_cache.shape, jnp.bfloat16),
            pltpu.VMEM((width // HD, HD), jnp.float32),
            pltpu.VMEM((1, resp), jnp.int32),
            pltpu.VMEM((1, resp), jnp.int32),
            pltpu.SMEM((1, slots), jnp.int32),
            pltpu.VMEM((2, prefix_len, kv_width), jnp.bfloat16),
            pltpu.VMEM((2, slots * rows, kv_width), jnp.bfloat16),
            pltpu.VMEM((2, slots * rows, kv_width), jnp.bfloat16),
            pltpu.VMEM(queries.shape, jnp.bfloat16),
            pltpu.VMEM(queries.shape, jnp.bfloat16),
            pltpu.VMEM(queries.shape, jnp.bfloat16),
            near,
            near,
            near,
            near,
            pltpu.VMEM((slots, chunks, keys, HD), jnp.float32),
            pltpu.VMEM((slots, kv_heads, LAST_ROWS, keys), jnp.bfloat16),
            pltpu.VMEM((slots, kv_heads, LAST_ROWS, keys), jnp.float32),
            pltpu.VMEM((slots, kv_heads, LAST_ROWS, HD), jnp.float32),
            pltpu.VMEM((slots, kv_heads, LAST_ROWS, HD), jnp.bfloat16),
            pltpu.VMEM((slots, kv_heads, LAST_ROWS, HD), jnp.float32),
            pltpu.VMEM((8, HD), jnp.float32),
            pltpu.VMEM((n_all, 8, HD), jnp.float32),
            pltpu.VMEM((n_dp * 8, HD), jnp.float32),
            pltpu.VMEM((2, kv_heads, 2 * group, HD), jnp.bfloat16),
            pltpu.VMEM((4, 2, kv_heads, 2 * group, HD), jnp.bfloat16),
            pltpu.VMEM((2 * group, HD), jnp.float32),
            pltpu.VMEM((4, 2 * group, HD), jnp.float32),
            pltpu.VMEM((2 * group, HD), jnp.float32),
            block,
            block,
            block,
            block,
            block,
            block,
            block,
            block,
            pltpu.SemaphoreType.DMA((9,)),
            pltpu.SemaphoreType.DMA((chunks, 4)),
            pltpu.SemaphoreType.DMA((chunks, 4)),
            pltpu.SemaphoreType.DMA((chunks, 4)),
            pltpu.SemaphoreType.DMA((chunks, 4)),
            pltpu.SemaphoreType.DMA((n_all,)),
            pltpu.SemaphoreType.DMA((n_all,)),
            pltpu.SemaphoreType.DMA((2, 4)),
            pltpu.SemaphoreType.DMA((2, 4)),
        ],
        compiler_params=pltpu.CompilerParams(
            collective_id=0, has_side_effects=True, vmem_limit_bytes=60 * 1024 * 1024
        ),
    )(
        slot_offsets,
        queries,
        upstream,
        prefix_cache,
        response_cache,
        reward_probe.reshape(width // HD, HD),
        partner.reshape(1, resp),
        labels.reshape(1, resp),
    )
    results = [rewards, loss, grad_q, grad_r, grad_p]
    moved = (0, 1, 2, 3, 4)
    taken = [results[i] for i in moved]
    given = pl.pallas_call(
        hand_over,
        out_shape=tuple(jax.ShapeDtypeStruct(x.shape, x.dtype) for x in taken),
        in_specs=[smem if x.ndim == 1 else vmem for x in taken],
        out_specs=tuple(smem if x.ndim == 1 else vmem for x in taken),
    )(*taken)
    for i, value in zip(moved, given):
        results[i] = value
    return tuple(results)


def solution(mesh):
    in_specs = (
        P(("group", "dp"), None, "tensor"),
        P(("group", "dp"), None, None, "tensor"),
        P(("group", "dp"), None, None, "tensor"),
        P(("group", "dp"), None, "tensor"),
        P("tensor"),
        P(("group", "dp"), None),
        P("group"),
        P("group"),
    )
    out_specs = (
        P(("group", "dp")),
        P("group"),
        P(("group", "dp"), None, "tensor"),
        P(("group", "dp"), None, None, "tensor"),
        P(("group", "dp"), None, None, "tensor"),
    )
    return jax.shard_map(
        functools.partial(per_device, mesh.shape["dp"], mesh.shape["tensor"]),
        mesh=mesh,
        in_specs=in_specs,
        out_specs=out_specs,
        check_vma=False,
    )
```
